256 devices in a mesh: dp: 16 (over y, z_hi), tp: 16 (over x, z_lo, core).
Axes of the slice: x: 4, y: 4, z: 8 (z_hi: 4, z_lo: 2; z = z_hi * 2 + z_lo), core: 2. Of those that a mesh axis runs over, the one named last changes fastest.
Arguments:
- inputs: bfloat16 [12288, 8192], P('dp', 'tp'), may hold values from -6 to 6
- gate_pre: bfloat16 [12288, 14336], P('dp', 'tp'), may hold values from -6 to 6
- up_pre: bfloat16 [12288, 14336], P('dp', 'tp'), may hold values from -6 to 6
- out_grads: bfloat16 [12288, 8192], P('dp', 'tp'), may hold values from -6 to 6
- down_weight: bfloat16 [14336, 8192], P('tp', 'dp'), may hold values from -0.0625 to 0.0625
- example_ids: int32 [12288], P('dp'), may hold values from 0 to 63, as said below
- input_factor: bfloat16 [8192, 64], P('tp'), may hold values from -0.5 to 0.5
- gate_factor: bfloat16 [14336, 64], P('tp'), may hold values from -0.5 to 0.5
- up_factor: bfloat16 [14336, 64], P('tp'), may hold values from -0.5 to 0.5
- hidden_factor: bfloat16 [14336, 64], P('tp'), may hold values from -0.5 to 0.5
- output_factor: bfloat16 [8192, 64], replicated, may hold values from -0.5 to 0.5
- queries: bfloat16 [8192, 4096], P(('dp', 'tp')), may hold values from -6 to 6
Outputs:
- scores: float32 [64, 8192], P(None, ('dp', 'tp'))
The draws below stay inside these ranges and needn't reach their ends.
Inputs may be any that keep to these rules, and one draw needn't show every extreme that they name: `example_ids`: the tokens of index b of dp carry the example ids b * 4 to b * 4 + 3, never falling along the tokens, each id on at least one token.
All inputs are finite; a program needn't handle non-finite values.
Results may differ from the reference program's by a relative error of at most 0.0029.
Values may be sent and summed in bfloat16 or wider, within the bound.
A program may use at most 128 MiB of HBM per device.

```python
import math
import jax
import jax.numpy as jnp
from jax import lax

D = 8192
FF = 14336
R = 64
TOK_DEV = 768
EX_DEV = 4
TOKENS = 12288
EXAMPLES = 64
QUERIES = 8192
N_DP = 16


def factor_draw(key, rows, top_scale):
    value_key = jax.random.fold_in(key, 0)
    scale_key = jax.random.fold_in(key, 2)
    normal_part = jax.random.truncated_normal(value_key, -4.0, 4.0, (rows, R), jnp.float32)
    log_scale = jax.random.uniform(scale_key, (1, R), jnp.float32, 0.0, math.log(top_scale))
    values = normal_part
    return (values * jnp.exp(log_scale) / math.sqrt(max(rows, 8192))).astype(jnp.bfloat16)


def draw_example_ids(key, part):
    key = jax.random.fold_in(key, 5)
    blocks = TOKENS // TOK_DEV
    block_keys = jax.random.split(key, blocks)

    def one_block(block_key):
        shuffled = jax.random.permutation(block_key, TOK_DEV - 1) + 1
        cut_points = jnp.sort(shuffled[:EX_DEV - 1])
        positions = jnp.arange(TOK_DEV, dtype=jnp.int32)
        return jnp.sum((positions[:, None] >= cut_points[None, :]).astype(jnp.int32), axis=1)
    local_ids = jax.vmap(one_block)(block_keys)
    offsets = (jnp.arange(blocks, dtype=jnp.int32) * EX_DEV)[:, None]
    return (local_ids + offsets).reshape(TOKENS).astype(jnp.int32)


def draw_input_factor(key, part):
    key = jax.random.fold_in(key, 21)
    return factor_draw(key, D, 10.0)


def draw_gate_factor(key, part):
    key = jax.random.fold_in(key, 22)
    return factor_draw(key, FF, 10.0)


def draw_up_factor(key, part):
    key = jax.random.fold_in(key, 23)
    return factor_draw(key, FF, 10.0)


def draw_hidden_factor(key, part):
    key = jax.random.fold_in(key, 24)
    return factor_draw(key, FF, 10.0)


def draw_output_factor(key, part):
    key = jax.random.fold_in(key, 25)
    return factor_draw(key, D, 10.0)


def block_levels(key, dims, pieces, smallest, top_value):
    factor_of = 1.0
    for dim, parts in pieces:
        steps = jax.random.uniform(jax.random.fold_in(jax.random.fold_in(key, 6), dim), (parts,), jnp.float32, smallest / len(pieces), top_value / len(pieces))
        factor_of = factor_of * jnp.repeat(jnp.exp(steps), dims[dim] // parts).reshape((-1,) + (1,) * (len(dims) - 1 - dim))
    return factor_of


def noise(key, shape, scale, reach, pieces=(), held_as=jnp.bfloat16):
    entries = jax.random.normal(key, shape, jnp.float32) * scale
    if len(pieces) > 0:
        entries = block_levels(key, shape, pieces, -0.22, 0.18) * entries
    return jnp.clip(entries, min=-reach, max=reach).astype(held_as)


def setup_inputs(seed: int = 0) -> dict:
    keys = jax.random.split(jax.random.key(seed), 13)
    inputs = noise(keys[0], (TOKENS, D), 1.0, 6.0, ((0, 16), (1, 16)))
    gate_pre = noise(keys[1], (TOKENS, FF), 1.0, 6.0, ((0, 16), (1, 16)))
    up_pre = noise(keys[2], (TOKENS, FF), 1.0, 6.0, ((0, 16), (1, 16)))
    out_grads = noise(keys[3], (TOKENS, D), 1.0, 6.0, ((0, 16), (1, 16)))
    down_weight = noise(keys[4], (FF, D), D ** -0.5, 0.0625, ((0, 16), (1, 16)))
    example_ids = draw_example_ids(jax.random.fold_in(keys[12], 71), 0)
    input_factor = draw_input_factor(jax.random.fold_in(keys[12], 71), 0)
    gate_factor = draw_gate_factor(jax.random.fold_in(keys[12], 71), 0)
    up_factor = draw_up_factor(jax.random.fold_in(keys[12], 71), 0)
    hidden_factor = draw_hidden_factor(jax.random.fold_in(keys[12], 71), 0)
    output_factor = draw_output_factor(jax.random.fold_in(keys[12], 71), 0)
    queries = noise(keys[11], (QUERIES, R * R), 1.0, 6.0, ((0, 256),))
    return {"inputs": inputs, "gate_pre": gate_pre, "up_pre": up_pre, "out_grads": out_grads, "down_weight": down_weight, "example_ids": example_ids, "input_factor": input_factor, "gate_factor": gate_factor, "up_factor": up_factor, "hidden_factor": hidden_factor, "output_factor": output_factor, "queries": queries}


def outer_sums(member_mask, left_proj, right_proj):
    return jnp.einsum('et,ti,tj->eij', member_mask, left_proj, right_proj, precision=lax.Precision.HIGHEST)

def reference(inputs, gate_pre, up_pre, out_grads, down_weight, example_ids, input_factor, gate_factor, up_factor, hidden_factor, output_factor, queries):
    gate_table = gate_factor.astype(jnp.float32)
    up_table = up_factor.astype(jnp.float32)
    hidden_table = hidden_factor.astype(jnp.float32)

    def one_block(packed):
        block_index, input_rows, gate_rows, up_rows, grad_rows, id_rows = packed
        hidden_grad = jnp.dot(grad_rows, down_weight.T, preferred_element_type=jnp.float32)
        gate_values = gate_rows.astype(jnp.float32)
        up_values = up_rows.astype(jnp.float32)
        gate_sigmoid = jax.nn.sigmoid(gate_values)
        activated = gate_values * gate_sigmoid
        hidden = activated * up_values
        gate_grad = hidden_grad * up_values * gate_sigmoid * (1.0 + gate_values * (1.0 - gate_sigmoid))
        up_grad = hidden_grad * activated
        input_proj = jnp.dot(input_rows, input_factor, preferred_element_type=jnp.float32)
        output_proj = jnp.dot(grad_rows, output_factor, preferred_element_type=jnp.float32)
        grad_proj = jnp.dot(gate_grad, gate_table, precision=lax.Precision.HIGHEST) + jnp.dot(up_grad, up_table, precision=lax.Precision.HIGHEST)
        hidden_proj = jnp.dot(hidden, hidden_table, precision=lax.Precision.HIGHEST)
        wanted = block_index * EX_DEV + jnp.arange(EX_DEV, dtype=jnp.int32)
        member_mask = (id_rows[None, :] == wanted[:, None]).astype(jnp.float32)
        sketch = outer_sums(member_mask, input_proj, grad_proj) + outer_sums(member_mask, hidden_proj, output_proj)
        return sketch.reshape(EX_DEV, R * R)
    packed = (jnp.arange(N_DP, dtype=jnp.int32), inputs.reshape(N_DP, TOK_DEV, D), gate_pre.reshape(N_DP, TOK_DEV, FF), up_pre.reshape(N_DP, TOK_DEV, FF), out_grads.reshape(N_DP, TOK_DEV, D), example_ids.reshape(N_DP, TOK_DEV))
    sketches = lax.map(one_block, packed).reshape(EXAMPLES, R * R)
    mean_square = lax.optimization_barrier(jnp.mean(sketches * sketches, axis=1, keepdims=True))
    unit_sketch = (sketches * lax.rsqrt(mean_square + 1e-06)).astype(jnp.bfloat16)
    products = lax.dot_general(unit_sketch, queries, (((1,), (1,)), ((), ())), preferred_element_type=jnp.float32)
    return products * (1.0 / R)
```

```python
import functools

import jax
import jax.numpy as jnp
from jax import lax
from jax.experimental import pallas as pl
from jax.experimental.pallas import tpu as pltpu
from jax.sharding import PartitionSpec as P

TOK = 768
DS = 512
FS = 896
CH = 128
NCH = FS // CH
HALF = CH // 2
N = 16
MESH = pl.DeviceIdType.MESH
HIGHEST = lax.Precision.HIGHEST
NT = (((1,), (1,)), ((), ()))


def dot(a, b, precision=None):
    return jnp.dot(a, b, preferred_element_type=jnp.float32, precision=precision)


def dot_nt(a, b, precision=None):
    return lax.dot_general(a, b, NT, preferred_element_type=jnp.float32, precision=precision)


def split(x):
    hi = x.astype(jnp.bfloat16)
    lo = (x - hi.astype(jnp.float32)).astype(jnp.bfloat16)
    return hi, lo


def iota2(shape):
    return (
        lax.broadcasted_iota(jnp.int32, shape, 0),
        lax.broadcasted_iota(jnp.int32, shape, 1),
    )


def spread(kind):
    row, col = iota2((64, 128))
    hit = (row == ((col >> 3) << 2) + (col & 3)) & (((col >> 2) & 1) == kind)
    return jnp.where(hit, 1.0, 0.0).astype(jnp.bfloat16)


def kernel(
    in_hbm, gate_hbm, up_hbm, og_hbm, w_hbm, ids_ref, inf_ref, gf_ref, uf_ref, hf_ref, of_hbm, q_hbm,
    out_ref,
    ogb, wb, inb, gb, ub, ofb, qb, ab, fp, acc, pih_msg, pih_rcv, iph, opt, gmat, omat, t2,
    gacc, gmsg, grcv, pall, qj, scm, scr,
    loc_sem, zs_s, zs_r, ys_s, ys_r, oz_s, oz_r, ox_s, ox_r, oc_s, oc_r, small_s, small_r,
):
    dp, tp = lax.axis_index("dp"), lax.axis_index("tp")
    x, zl, core = tp >> 2, (tp >> 1) & 1, tp & 1
    y, zh = dp >> 2, dp & 3

    def dev(d, t):
        return {"dp": d, "tp": t}

    def remote(src, dst, ss, rs, d, t):
        return pltpu.make_async_remote_copy(
            src_ref=src, dst_ref=dst, send_sem=ss, recv_sem=rs,
            device_id=dev(d, t), device_id_type=MESH,
        )

    pending = []

    def send(src, dst, ss, rs, d, t):
        copy = remote(src, dst, ss, rs, d, t)
        copy.start()
        pending.append(copy)

    def arrived(dst, rs):
        remote(dst, dst, rs, rs, dp, tp ^ 1).wait_recv()

    loads = []
    for n, (src, dst) in enumerate((
        (w_hbm, wb.at[dp]), (og_hbm, ogb.at[tp]), (in_hbm, inb), (gate_hbm, gb), (up_hbm, ub),
        (q_hbm, qb), (of_hbm, ofb),
    )):
        copy = pltpu.make_async_copy(src, dst, loc_sem.at[n])
        copy.start()
        loads.append(copy)
    barrier = pltpu.get_barrier_semaphore()
    for k in range(1, N):
        pl.semaphore_signal(barrier, 1, device_id=dev(dp, tp ^ k), device_id_type=MESH)
        pl.semaphore_signal(barrier, 1, device_id=dev(dp ^ k, tp), device_id_type=MESH)
    pl.semaphore_wait(barrier, 2 * (N - 1))
    loads[0].wait()
    loads[1].wait()

    zh_up, zh_down = (zh + 1) & 3, (zh + 3) & 3
    y_up, y_down = (y + 1) & 3, (y + 3) & 3
    zh_of = (zh, zh_down, zh_up, (zh + 2) & 3)

    def at(yy, zz):
        return yy * 4 + zz

    def rows(i, part=None):
        if part is None:
            return pl.ds(i * CH, CH)
        return pl.ds(i * CH + part * HALF, HALF)

    def w_send(block, r, sems, idx, target):
        ss, rs = sems
        ref = wb.at[block, r]
        send(ref, ref, ss.at[idx], rs.at[idx], target, tp)

    def z_own(i):
        w_send(dp, rows(i), (zs_s, zs_r), 4 * i, at(y, zh_up))
        w_send(dp, rows(i), (zs_s, zs_r), 4 * i + 1, at(y, zh_down))

    def z_forward(i):
        arrived(wb.at[at(y, zh_down), rows(i)], zs_r.at[4 * i])
        w_send(at(y, zh_down), rows(i, 0), (zs_s, zs_r), 4 * i + 2, at(y, zh_up))
        arrived(wb.at[at(y, zh_up), rows(i)], zs_r.at[4 * i + 1])
        w_send(at(y, zh_up), rows(i, 1), (zs_s, zs_r), 4 * i + 3, at(y, zh_down))

    def z_last(i):
        for part in range(2):
            arrived(wb.at[at(y, zh_of[3]), rows(i, part)], zs_r.at[4 * i + 2 + part])

    def y_send(i, q):
        base = 16 * i + 4 * q
        w_send(at(y, zh_of[q]), rows(i), (ys_s, ys_r), base, at(y_up, zh))
        w_send(at(y, zh_of[q]), rows(i), (ys_s, ys_r), base + 1, at(y_down, zh))

    def y_forward(i, q):
        base = 16 * i + 4 * q
        arrived(wb.at[at(y_down, zh_of[q]), rows(i)], ys_r.at[base])
        w_send(at(y_down, zh_of[q]), rows(i, 0), (ys_s, ys_r), base + 2, at(y_up, zh))
        arrived(wb.at[at(y_up, zh_of[q]), rows(i)], ys_r.at[base + 1])
        w_send(at(y_up, zh_of[q]), rows(i, 1), (ys_s, ys_r), base + 3, at(y_down, zh))

    def y_last(i, q):
        base = 16 * i + 4 * q
        for part in range(2):
            arrived(wb.at[at((y + 2) & 3, zh_of[q]), rows(i, part)], ys_r.at[base + 2 + part])

    x_up, x_down, x_far = (x + 1) & 3, (x + 3) & 3, (x + 2) & 3

    def tat(xx, zz, cc):
        return xx * 4 + zz * 2 + cc

    zl_of = (zl, 1 - zl)

    def o_core(slot, idx):
        send(ogb.at[slot], ogb.at[slot], oc_s.at[idx], oc_r.at[idx], dp, tp ^ 1)

    def o_x(q):
        slot = tat(x, zl_of[q], core)
        send(ogb.at[slot], ogb.at[slot], ox_s.at[4 * q], ox_r.at[4 * q], dp, tat(x_up, zl, core))
        send(ogb.at[slot], ogb.at[slot], ox_s.at[4 * q + 1], ox_r.at[4 * q + 1], dp, tat(x_down, zl, core))

    def o_part(slot, part):
        return ogb.at[slot, pl.ds(part * (TOK // 2), TOK // 2)]

    def o_forward(q):
        slot = tat(x_down, zl_of[q], core)
        arrived(ogb.at[slot], ox_r.at[4 * q])
        ref = o_part(slot, 0)
        send(ref, ref, ox_s.at[4 * q + 2], ox_r.at[4 * q + 2], dp, tat(x_up, zl, core))
        o_core(slot, 2 + 3 * q)
        slot = tat(x_up, zl_of[q], core)
        arrived(ogb.at[slot], ox_r.at[4 * q + 1])
        ref = o_part(slot, 1)
        send(ref, ref, ox_s.at[4 * q + 3], ox_r.at[4 * q + 3], dp, tat(x_down, zl, core))
        o_core(slot, 3 + 3 * q)

    def o_last(q):
        slot = tat(x_far, zl_of[q], core)
        for part in range(2):
            arrived(o_part(slot, part), ox_r.at[4 * q + 2 + part])
        o_core(slot, 4 + 3 * q)

    def o_all():
        other = 1 - core
        arrived(ogb.at[tat(x, zl, other)], oc_r.at[0])
        arrived(ogb.at[tat(x, 1 - zl, other)], oc_r.at[1])
        for q in range(2):
            for k, xx in enumerate((x_down, x_up, x_far)):
                arrived(ogb.at[tat(xx, zl_of[q], other)], oc_r.at[2 + 3 * q + k])

    def exchange(idx, src_of, dst_of, axis):
        for k in range(1, N):
            d, t = (dp ^ k, tp) if axis == "dp" else (dp, tp ^ k)
            peer = d if axis == "dp" else t
            remote(src_of(peer), dst_of(k), small_s.at[idx], small_r.at[idx], d, t).start()

    def exchanged(idx, fifteen):
        copy = remote(fifteen, fifteen, small_s.at[idx], small_r.at[idx], dp, tp ^ 1)
        copy.wait_recv()
        copy.wait_send()

    z_own(0)
    send(ogb.at[tp], ogb.at[tp], oz_s, oz_r, dp, tat(x, 1 - zl, core))
    o_x(0)
    y_send(0, 0)
    o_core(tp, 0)
    z_own(1)
    y_send(1, 0)
    z_own(2)
    y_send(2, 0)

    def early():
        for n in range(2, 6):
            loads[n].wait()
        exchange(1, lambda peer: qb.at[peer], lambda k: qj.at[tp], "tp")
        sel0, sel1 = spread(0), spread(1)
        acc[...] = dot(inb[...], dot(inf_ref[...], sel0).astype(jnp.bfloat16))

        @pl.loop(0, NCH)
        def _(i):
            lanes = pl.ds(pl.multiple_of(i * CH, CH), CH)
            frows = pl.ds(pl.multiple_of(i * CH, CH), CH)
            g = gb[:, lanes].astype(jnp.float32)
            u = ub[:, lanes].astype(jnp.float32)
            s = jax.nn.sigmoid(g)
            activated = g * s
            ab[i, :, :CH] = u * s * (1.0 + g * (1.0 - s))
            ab[i, :, CH:] = activated
            hi, lo = split(activated * u)
            hfp = dot(hf_ref[frows, :], sel1).astype(jnp.bfloat16)
            acc[...] += dot(hi, hfp) + dot(lo, hfp)
            for h, sel in enumerate((sel0, sel1)):
                fp[h, i, :CH, :] = dot(gf_ref[frows, :], sel).astype(jnp.bfloat16)
                fp[h, i, CH:, :] = dot(uf_ref[frows, :], sel).astype(jnp.bfloat16)

        pih_msg[...] = acc[...].T.reshape(N, 8, TOK)
        exchange(0, lambda peer: pih_msg.at[peer], lambda k: pih_rcv.at[k - 1], "tp")

    def middle():
        exchanged(0, pih_rcv)
        total = pih_msg[tp]
        for k in range(N - 1):
            total = total + pih_rcv[k]
        iph[tp] = total
        exchange(2, lambda peer: iph.at[tp], lambda k: iph.at[tp], "tp")

    def mask():
        row, _ = iota2((4, TOK))
        return jnp.where(ids_ref[...] == dp * 4 + row, 1.0, 0.0)

    def by_example(dst, cols):
        m = mask()
        for jl in range(2):
            for jh in range(2):
                r = 8 * jl + 4 * jh
                jj = 2 * jh + jl
                dst[r : r + 4, :] = m * cols[jj : jj + 1, :]

    def iph2():
        return iph[...].reshape(N * 8, TOK)

    def output_side():
        loads[6].wait()
        sel0 = spread(0)
        acc[...] = jnp.zeros_like(acc)

        @pl.loop(0, N)
        def _(k):
            ofp = dot(ofb[pl.ds(pl.multiple_of(k * DS, DS), DS), :], sel0).astype(jnp.bfloat16)
            acc[...] += dot(ogb[k], ofp)

        opt[...] = acc[...].T.reshape(N, 8, TOK)
        by_example(omat, opt[tp])
        exchanged(2, iph.at[pl.ds(0, N - 1)])
        t2[...] = dot_nt(omat[...], iph2(), HIGHEST)
        exchanged(1, qj.at[pl.ds(0, N - 1)])
        qj[tp] = qb[tp]
        gacc[...] = jnp.zeros_like(gacc)

    def compute(i):
        for q in range(4):
            y_last(i, q)
        acc[...] = jnp.zeros_like(acc)

        @pl.loop(0, N)
        def _(k):
            acc[...] += dot_nt(ogb[k], wb[k, rows(i), :])

        for h in range(2):
            tok = slice(h * (TOK // 2), (h + 1) * (TOK // 2))
            c = acc[tok, :]
            hi_g, lo_g = split(c * ab[i, tok, :CH])
            hi_u, lo_u = split(c * ab[i, tok, CH:])
            gacc[...] += (
                dot(hi_g, fp[h, i, :CH, :]) + dot(lo_g, fp[h, i, :CH, :])
                + dot(hi_u, fp[h, i, CH:, :]) + dot(lo_u, fp[h, i, CH:, :])
            )

    early()
    for i in range(NCH + 3):
        if i < NCH:
            z_forward(i)
            y_send(i, 1)
            y_send(i, 2)
            if i + 3 < NCH:
                z_own(i + 3)
                y_send(i + 3, 0)
        if i == 0:
            slot = tat(x, 1 - zl, core)
            arrived(ogb.at[slot], oz_r)
            o_x(1)
            o_core(slot, 1)
        if i == 1:
            o_forward(0)
            middle()
        if i == 2:
            o_forward(1)
            o_last(0)
        if i == 3:
            o_last(1)
        if 1 <= i <= NCH:
            z_last(i - 1)
            y_send(i - 1, 3)
            for q in range(3):
                y_forward(i - 1, q)
        if 2 <= i <= NCH + 1:
            y_forward(i - 2, 3)
        if i == 3:
            o_all()
            output_side()
        if i >= 3:
            compute(i - 3)

    gmsg[...] = gacc[...].T.reshape(N, 8, TOK // 2)
    exchange(3, lambda peer: gmsg.at[peer], lambda k: grcv.at[k - 1], "tp")
    for copy in pending:
        copy.wait_send()
    exchanged(3, grcv)
    total = gmsg[tp]
    for k in range(N - 1):
        total = total + grcv[k]
    by_example(gmat, jnp.concatenate([total[0:4, :], total[4:8, :]], axis=1))
    t1 = dot_nt(gmat[...], iph2(), HIGHEST)
    _, lane = iota2((16, 128))
    both = jnp.where(((lane >> 2) & 1) == 0, t1, t2[...])
    row, col = iota2((128, 128))
    feature = ((row >> 3) << 2) + (row & 3)
    piece = jnp.zeros((8, 128), jnp.float32)
    for jl in range(2):
        place = jnp.where(col == jl * 64 + feature, 1.0, 0.0)
        piece = piece + dot(both[8 * jl : 8 * jl + 8, :], place, HIGHEST)
    pall[dp] = piece
    exchange(4, lambda peer: pall.at[dp], lambda k: pall.at[dp], "dp")
    exchanged(4, pall.at[pl.ds(0, N - 1)])
    sketch = pall[...].reshape(128, 128)
    hi, lo = split(sketch)
    squares = dot_nt(jnp.ones((8, 128), jnp.float32), sketch * sketch, HIGHEST)
    r = []
    for jh in range(2):
        qq = qj[:, :, 128 * jh : 128 * jh + 128].reshape(N * 32, 128)
        r.append(dot_nt(qq, hi) + dot_nt(qq, lo))
    _, lane = iota2((N * 32, 128))
    part = jnp.where(((lane >> 2) & 1) == 0, r[0], r[1])
    scm[:, 0:32, :] = part.reshape(N, 32, 128)
    scm[:, 32:40, :] = jnp.broadcast_to(squares[None], (N, 8, 128))
    exchange(5, lambda peer: scm.at[peer], lambda k: scr.at[k - 1], "tp")
    exchanged(5, scr)
    total = scm[tp]
    for k in range(N - 1):
        total = total + scr[k]
    row, col = iota2((64, 128))
    pick = jnp.where(((row >> 2) == (col >> 3)) & ((row & 3) == (col & 3)), 1.0, 0.0)
    full = dot_nt(pick, total, HIGHEST)
    scale = lax.rsqrt(full[:, 32:33] * (1.0 / 4096.0) + 1e-06) * (1.0 / 64.0)
    out_ref[...] = full[:, 0:32] * scale


def local(
    inputs, gate_pre, up_pre, out_grads, down_weight, example_ids,
    input_factor, gate_factor, up_factor, hidden_factor, output_factor, queries,
):
    by_column = queries.reshape(32, 64, N, 4).transpose(2, 0, 3, 1).reshape(N, 32, 256)
    hbm = pl.BlockSpec(memory_space=pl.ANY)
    vmem = pl.BlockSpec(memory_space=pltpu.VMEM)
    bf16, f32 = jnp.bfloat16, jnp.float32
    dma = pltpu.SemaphoreType.DMA
    return pl.pallas_call(
        kernel,
        out_shape=jax.ShapeDtypeStruct((64, 32), f32),
        in_specs=[hbm, hbm, hbm, hbm, hbm, vmem, vmem, vmem, vmem, vmem, hbm, hbm],
        out_specs=vmem,
        scratch_shapes=[
            pltpu.VMEM((N, TOK, DS), bf16),
            pltpu.VMEM((N, FS, DS), bf16),
            pltpu.VMEM((TOK, DS), bf16),
            pltpu.VMEM((TOK, FS), bf16),
            pltpu.VMEM((TOK, FS), bf16),
            pltpu.VMEM((N * DS, 64), bf16),
            pltpu.VMEM((N, 32, 256), bf16),
            pltpu.VMEM((NCH, TOK, 2 * CH), f32),
            pltpu.VMEM((2, NCH, 2 * CH, 128), bf16),
            pltpu.VMEM((TOK, 128), f32),
            pltpu.VMEM((N, 8, TOK), f32),
            pltpu.VMEM((N - 1, 8, TOK), f32),
            pltpu.VMEM((N, 8, TOK), f32),
            pltpu.VMEM((N, 8, TOK), f32),
            pltpu.VMEM((16, TOK), f32),
            pltpu.VMEM((16, TOK), f32),
            pltpu.VMEM((16, 128), f32),
            pltpu.VMEM((TOK // 2, 128), f32),
            pltpu.VMEM((N, 8, TOK // 2), f32),
            pltpu.VMEM((N - 1, 8, TOK // 2), f32),
            pltpu.VMEM((N, 8, 128), f32),
            pltpu.VMEM((N, 32, 256), bf16),
            pltpu.VMEM((N, 40, 128), f32),
            pltpu.VMEM((N - 1, 40, 128), f32),
            dma((7,)),
            dma((4 * NCH,)),
            dma((4 * NCH,)),
            dma((16 * NCH,)),
            dma((16 * NCH,)),
            dma,
            dma,
            dma((8,)),
            dma((8,)),
            dma((8,)),
            dma((8,)),
            dma((6,)),
            dma((6,)),
        ],
        compiler_params=pltpu.CompilerParams(
            collective_id=0, has_side_effects=True, vmem_limit_bytes=60 * 1024 * 1024
        ),
        cost_estimate=pl.CostEstimate(
            flops=2 * TOK * FS * N * DS, bytes_accessed=8 * 1024 * 1024, transcendentals=TOK * FS
        ),
        name="gather_and_score",
    )(
        inputs, gate_pre, up_pre, out_grads, down_weight, example_ids.reshape(1, TOK),
        input_factor, gate_factor, up_factor, hidden_factor, output_factor, by_column,
    )


def solution(mesh):
    return jax.shard_map(
        local,
        mesh=mesh,
        in_specs=(
            P("dp", "tp"),
            P("dp", "tp"),
            P("dp", "tp"),
            P("dp", "tp"),
            P("tp", "dp"),
            P("dp"),
            P("tp", None),
            P("tp", None),
            P("tp", None),
            P("tp", None),
            P(),
            P(("dp", "tp"), None),
        ),
        out_specs=P(None, ("dp", "tp")),
        check_vma=False,
    )
```

```python
import functools

import jax
import jax.numpy as jnp
from jax import lax
from jax.experimental import pallas as pl
from jax.experimental.pallas import tpu as pltpu
from jax.sharding import PartitionSpec as P

TOK = 768
DS = 512
FS = 896
CH = 128
NCH = FS // CH
YF = NCH - 1
YR = 96
START = (0, 128, 256, 384, 512, 768, 768 - YR)
LENGTH = (128, 128, 128, 128, 256 - YR, 128, YR)
N = 16
MESH = pl.DeviceIdType.MESH
HIGHEST = lax.Precision.HIGHEST
NT = (((1,), (1,)), ((), ()))


def dot(a, b, precision=None):
    return jnp.dot(a, b, preferred_element_type=jnp.float32, precision=precision)


def dot_nt(a, b, precision=None):
    return lax.dot_general(a, b, NT, preferred_element_type=jnp.float32, precision=precision)


def split(x):
    hi = x.astype(jnp.bfloat16)
    lo = (x - hi.astype(jnp.float32)).astype(jnp.bfloat16)
    return hi, lo


def iota2(shape):
    return (
        lax.broadcasted_iota(jnp.int32, shape, 0),
        lax.broadcasted_iota(jnp.int32, shape, 1),
    )


def spread(kind):
    row, col = iota2((128, 64))
    hit = (col == ((row >> 3) << 2) + (row & 3)) & (((row >> 2) & 1) == kind)
    return jnp.where(hit, 1.0, 0.0).astype(jnp.bfloat16)


def kernel(
    in_hbm, gate_hbm, up_hbm, og_hbm, w_hbm, ids_ref, inf_ref, gf_ref, uf_ref, hf_ref, of_hbm, q_hbm,
    out_ref,
    ogb, wb, inb, gb, ub, ofb, qn, qt, qb, ab, fp, acc, acc2, pih_msg, pih_rcv, iph, opt, gmat, omat, t2,
    gacc, gmsg, grcv, pall, qj, scm, scr,
    loc_sem, zs_s, zs_r, ys_s, ys_r, oz_s, oz_r, ox_s, ox_r, oc_s, oc_r, small_s, small_r,
):
    dp, tp = lax.axis_index("dp"), lax.axis_index("tp")
    x, zl, core = tp >> 2, (tp >> 1) & 1, tp & 1
    y, zh = dp >> 2, dp & 3

    def dev(d, t):
        return {"dp": d, "tp": t}

    def remote(src, dst, ss, rs, d, t):
        return pltpu.make_async_remote_copy(
            src_ref=src, dst_ref=dst, send_sem=ss, recv_sem=rs,
            device_id=dev(d, t), device_id_type=MESH,
        )

    pending = []

    def send(src, dst, ss, rs, d, t):
        copy = remote(src, dst, ss, rs, d, t)
        copy.start()
        pending.append(copy)

    def arrived(dst, rs):
        remote(dst, dst, rs, rs, dp, tp ^ 1).wait_recv()

    loads = []
    for n, (src, dst) in enumerate((
        (w_hbm, wb.at[dp]), (og_hbm, ogb.at[tp]), (in_hbm, inb), (gate_hbm, gb), (up_hbm, ub),
        (q_hbm, qn), (of_hbm, ofb),
    )):
        copy = pltpu.make_async_copy(src, dst, loc_sem.at[n])
        copy.start()
        loads.append(copy)
    barrier = pltpu.get_barrier_semaphore()
    for k in range(1, N):
        pl.semaphore_signal(barrier, 1, device_id=dev(dp, tp ^ k), device_id_type=MESH)
        pl.semaphore_signal(barrier, 1, device_id=dev(dp ^ k, tp), device_id_type=MESH)
    pl.semaphore_wait(barrier, 2 * (N - 1))
    loads[0].wait()
    loads[1].wait()

    zh_up, zh_down = (zh + 1) & 3, (zh + 3) & 3
    y_up, y_down = (y + 1) & 3, (y + 3) & 3
    zh_of = (zh, zh_down, zh_up, (zh + 2) & 3)

    def at(yy, zz):
        return yy * 4 + zz

    def rows(i, part=None):
        if part is None:
            return pl.ds(START[i], LENGTH[i])
        return pl.ds(START[i] + part * (LENGTH[i] // 2), LENGTH[i] // 2)

    def w_send(block, r, sems, idx, target):
        ss, rs = sems
        ref = wb.at[block, r]
        send(ref, ref, ss.at[idx], rs.at[idx], target, tp)

    def z_own(i):
        w_send(dp, rows(i), (zs_s, zs_r), 4 * i, at(y, zh_up))
        w_send(dp, rows(i), (zs_s, zs_r), 4 * i + 1, at(y, zh_down))

    def z_forward(i):
        arrived(wb.at[at(y, zh_down), rows(i)], zs_r.at[4 * i])
        w_send(at(y, zh_down), rows(i, 0), (zs_s, zs_r), 4 * i + 2, at(y, zh_up))
        arrived(wb.at[at(y, zh_up), rows(i)], zs_r.at[4 * i + 1])
        w_send(at(y, zh_up), rows(i, 1), (zs_s, zs_r), 4 * i + 3, at(y, zh_down))

    def z_last(i):
        for part in range(2):
            arrived(wb.at[at(y, zh_of[3]), rows(i, part)], zs_r.at[4 * i + 2 + part])

    def y_send(i, q):
        base = 16 * i + 4 * q
        w_send(at(y, zh_of[q]), rows(i), (ys_s, ys_r), base, at(y_up, zh))
        w_send(at(y, zh_of[q]), rows(i), (ys_s, ys_r), base + 1, at(y_down, zh))

    def y_forward(i, q):
        base = 16 * i + 4 * q
        arrived(wb.at[at(y_down, zh_of[q]), rows(i)], ys_r.at[base])
        w_send(at(y_down, zh_of[q]), rows(i, 0), (ys_s, ys_r), base + 2, at(y_up, zh))
        arrived(wb.at[at(y_up, zh_of[q]), rows(i)], ys_r.at[base + 1])
        w_send(at(y_up, zh_of[q]), rows(i, 1), (ys_s, ys_r), base + 3, at(y_down, zh))

    def y_last(i, q):
        base = 16 * i + 4 * q
        for part in range(2):
            arrived(wb.at[at((y + 2) & 3, zh_of[q]), rows(i, part)], ys_r.at[base + 2 + part])

    y_of = (y, y_down, y_up, (y + 2) & 3)

    def yo_send():
        w_send(dp, rows(YF), (zs_s, zs_r), 4 * YF, at(y_up, zh))
        w_send(dp, rows(YF), (zs_s, zs_r), 4 * YF + 1, at(y_down, zh))

    def yo_forward():
        arrived(wb.at[at(y_down, zh), rows(YF)], zs_r.at[4 * YF])
        w_send(at(y_down, zh), rows(YF, 0), (zs_s, zs_r), 4 * YF + 2, at(y_up, zh))
        arrived(wb.at[at(y_up, zh), rows(YF)], zs_r.at[4 * YF + 1])
        w_send(at(y_up, zh), rows(YF, 1), (zs_s, zs_r), 4 * YF + 3, at(y_down, zh))

    def yo_last():
        for part in range(2):
            arrived(wb.at[at(y_of[3], zh), rows(YF, part)], zs_r.at[4 * YF + 2 + part])

    def zq_send(q):
        base = 16 * YF + 4 * q
        w_send(at(y_of[q], zh), rows(YF), (ys_s, ys_r), base, at(y, zh_up))
        w_send(at(y_of[q], zh), rows(YF), (ys_s, ys_r), base + 1, at(y, zh_down))

    def zq_forward(q):
        base = 16 * YF + 4 * q
        arrived(wb.at[at(y_of[q], zh_down), rows(YF)], ys_r.at[base])
        w_send(at(y_of[q], zh_down), rows(YF, 0), (ys_s, ys_r), base + 2, at(y, zh_up))
        arrived(wb.at[at(y_of[q], zh_up), rows(YF)], ys_r.at[base + 1])
        w_send(at(y_of[q], zh_up), rows(YF, 1), (ys_s, ys_r), base + 3, at(y, zh_down))

    def zq_last(q):
        base = 16 * YF + 4 * q
        for part in range(2):
            arrived(wb.at[at(y_of[q], zh_of[3]), rows(YF, part)], ys_r.at[base + 2 + part])

    x_up, x_down, x_far = (x + 1) & 3, (x + 3) & 3, (x + 2) & 3

    def tat(xx, zz, cc):
        return xx * 4 + zz * 2 + cc

    zl_of = (zl, 1 - zl)

    def o_core(slot, idx):
        send(ogb.at[slot], ogb.at[slot], oc_s.at[idx], oc_r.at[idx], dp, tp ^ 1)

    def o_x(q):
        slot = tat(x, zl_of[q], core)
        send(ogb.at[slot], ogb.at[slot], ox_s.at[4 * q], ox_r.at[4 * q], dp, tat(x_up, zl, core))
        send(ogb.at[slot], ogb.at[slot], ox_s.at[4 * q + 1], ox_r.at[4 * q + 1], dp, tat(x_down, zl, core))

    def o_part(slot, part):
        return ogb.at[slot, pl.ds(part * (TOK // 2), TOK // 2)]

    def o_forward(q):
        slot = tat(x_down, zl_of[q], core)
        arrived(ogb.at[slot], ox_r.at[4 * q])
        ref = o_part(slot, 0)
        send(ref, ref, ox_s.at[4 * q + 2], ox_r.at[4 * q + 2], dp, tat(x_up, zl, core))
        o_core(slot, 2 + 3 * q)
        slot = tat(x_up, zl_of[q], core)
        arrived(ogb.at[slot], ox_r.at[4 * q + 1])
        ref = o_part(slot, 1)
        send(ref, ref, ox_s.at[4 * q + 3], ox_r.at[4 * q + 3], dp, tat(x_down, zl, core))
        o_core(slot, 3 + 3 * q)

    def o_last(q):
        slot = tat(x_far, zl_of[q], core)
        for part in range(2):
            arrived(o_part(slot, part), ox_r.at[4 * q + 2 + part])
        o_core(slot, 4 + 3 * q)

    def o_all():
        other = 1 - core
        arrived(ogb.at[tat(x, zl, other)], oc_r.at[0])
        arrived(ogb.at[tat(x, 1 - zl, other)], oc_r.at[1])
        for q in range(2):
            for k, xx in enumerate((x_down, x_up, x_far)):
                arrived(ogb.at[tat(xx, zl_of[q], other)], oc_r.at[2 + 3 * q + k])

    def exchange(idx, src_of, dst_of, axis):
        for k in range(1, N):
            d, t = (dp ^ k, tp) if axis == "dp" else (dp, tp ^ k)
            peer = d if axis == "dp" else t
            remote(src_of(peer), dst_of(k), small_s.at[idx], small_r.at[idx], d, t).start()

    def exchanged(idx, fifteen):
        copy = remote(fifteen, fifteen, small_s.at[idx], small_r.at[idx], dp, tp ^ 1)
        copy.wait_recv()
        copy.wait_send()

    z_own(0)
    send(ogb.at[tp], ogb.at[tp], oz_s, oz_r, dp, tat(x, 1 - zl, core))
    o_x(0)
    y_send(0, 0)
    yo_send()
    o_core(tp, 0)
    z_own(1)
    for i in range(1, YF):
        y_send(i, 0)

    def early():
        for n in range(2, 5):
            loads[n].wait()
        sel0, sel1 = spread(0), spread(1)
        acc[...] = dot_nt(inb[...], dot(sel0, inf_ref[...]).astype(jnp.bfloat16))

        @pl.loop(0, NCH)
        def _(i):
            lanes = pl.ds(pl.multiple_of(i * CH, CH), CH)
            g = gb[:, lanes].astype(jnp.float32)
            u = ub[:, lanes].astype(jnp.float32)
            s = jax.nn.sigmoid(g)
            activated = g * s
            ab[i, :, :CH] = u * s * (1.0 + g * (1.0 - s))
            ab[i, :, CH:] = activated
            hi, lo = split(activated * u)
            hfp = dot(sel1, hf_ref[:, lanes]).astype(jnp.bfloat16)
            acc[...] += dot_nt(hi, hfp) + dot_nt(lo, hfp)
            for h, sel in enumerate((sel0, sel1)):
                fp[h, i, :, :CH] = dot(sel, gf_ref[:, lanes]).astype(jnp.bfloat16)
                fp[h, i, :, CH:] = dot(sel, uf_ref[:, lanes]).astype(jnp.bfloat16)

        pih_msg[...] = acc[...].T.reshape(N, 8, TOK)
        exchange(0, lambda peer: pih_msg.at[peer], lambda k: pih_rcv.at[k - 1], "tp")

    def spread_queries():
        loads[5].wait()
        row, col = iota2((128, 128))
        hit = col == ((row & 1) << 6) + ((row >> 3) << 2) + ((row >> 1) & 3)
        place = jnp.where(hit, 1.0, 0.0).astype(jnp.bfloat16)
        for m in range(32):
            moved = dot_nt(place, qn[:, 128 * m : 128 * m + 128])
            qt[:, 8 * m : 8 * m + 8, 0:32] = moved.reshape(N, 8, 32)

        @pl.loop(0, N)
        def _(k):
            for half in range(2):
                turned = qt[k, 128 * half : 128 * half + 128, :].T
                qb[k, :, 128 * half : 128 * half + 128] = turned[0:32, :].astype(jnp.bfloat16)

        exchange(1, lambda peer: qb.at[peer], lambda k: qj.at[tp], "tp")

    def middle():
        exchanged(0, pih_rcv)
        total = pih_msg[tp]
        for k in range(N - 1):
            total = total + pih_rcv[k]
        iph[tp] = total
        exchange(2, lambda peer: iph.at[tp], lambda k: iph.at[tp], "tp")

    def mask():
        row, _ = iota2((4, TOK))
        return jnp.where(ids_ref[...].reshape(1, TOK) == dp * 4 + row, 1.0, 0.0)

    def by_example(dst, cols):
        m = mask()
        for jj in range(4):
            dst[4 * jj : 4 * jj + 4, :] = m * cols[jj : jj + 1, :]

    def iph2():
        return iph[...].reshape(N * 8, TOK)

    def output_side():
        loads[6].wait()
        sel0 = spread(0)
        acc[...] = jnp.zeros_like(acc)

        @pl.loop(0, N)
        def _(k):
            ofp = dot(sel0, ofb[:, pl.ds(pl.multiple_of(k * DS, DS), DS)]).astype(jnp.bfloat16)
            acc[...] += dot_nt(ogb[k], ofp)

        opt[...] = acc[...].T.reshape(N, 8, TOK)
        by_example(omat, opt[tp])
        exchanged(2, iph.at[pl.ds(0, N - 1)])
        t2[...] = dot_nt(omat[...], iph2(), HIGHEST)
        exchanged(1, qj.at[pl.ds(0, N - 1)])
        qj[tp] = qb[tp]
        gacc[...] = jnp.zeros_like(gacc)

    def multiply(place, width, ks, first):
        out = acc2.at[:, pl.ds(0, width * CH)]
        if first:
            out[...] = jnp.zeros_like(out)

        @pl.loop(0, 4)
        def _(n):
            for k in ks:
                slot = k(n)
                out[...] += dot_nt(ogb[slot], wb[slot, pl.ds(place * CH, width * CH), :])

    def project(place, half):
        for h in range(2):
            tok = slice(h * (TOK // 2), (h + 1) * (TOK // 2))
            c = acc2[tok, half * CH : half * CH + CH]
            hi_g, lo_g = split(c * ab[place, tok, :CH])
            hi_u, lo_u = split(c * ab[place, tok, CH:])
            gacc[...] += (
                dot_nt(hi_g, fp[h, place, :, :CH]) + dot_nt(lo_g, fp[h, place, :, :CH])
                + dot_nt(hi_u, fp[h, place, :, CH:]) + dot_nt(lo_u, fp[h, place, :, CH:])
            )

    def slot_of(q):
        return lambda n: n * 4 + zh_of[q]

    every = [slot_of(q) for q in range(4)]

    def compute_pair(place):
        multiply(place, 2, every, True)
        project(place, 0)
        project(place + 1, 1)

    def y_wait(i, qs):
        for q in qs:
            y_last(i, q)

    early()
    for i in range(YF + 2):
        if i < YF:
            z_forward(i)
            y_send(i, 1)
            y_send(i, 2)
            if i + 2 < YF:
                z_own(i + 2)
        if 1 <= i <= YF:
            z_last(i - 1)
            y_send(i - 1, 3)
        if i == 0:
            yo_forward()
            for k in range(YF):
                y_forward(k, 0)
            o_forward(0)
        if 1 <= i <= YF:
            y_forward(i - 1, 1)
            y_forward(i - 1, 2)
        if 2 <= i <= YF + 1:
            y_forward(i - 2, 3)
        if i == 1:
            slot = tat(x, 1 - zl, core)
            arrived(ogb.at[slot], oz_r)
            o_x(1)
            o_core(slot, 1)
            middle()
            spread_queries()
        if i == 3:
            o_forward(1)
            o_last(0)
        if i == 4:
            yo_last()
            for q in range(4):
                zq_send(q)
            o_last(1)
            o_all()
            output_side()
        if i == 5:
            for q in range(4):
                zq_forward(q)
            y_wait(0, range(4))
            y_wait(1, range(4))
            compute_pair(0)
        if i == 6:
            y_wait(2, range(4))
            y_wait(3, range(4))
            compute_pair(2)
            y_wait(4, range(4))
            for q in range(4):
                zq_last(q)
            compute_pair(4)
    y_wait(5, range(3))
    multiply(6, 1, every[:3], True)
    y_wait(5, [3])
    multiply(6, 1, every[3:], False)
    project(6, 0)

    gmsg[...] = gacc[...].T.reshape(N, 8, TOK // 2)
    exchange(3, lambda peer: gmsg.at[peer], lambda k: grcv.at[k - 1], "tp")
    for copy in pending:
        copy.wait_send()
    exchanged(3, grcv)
    total = gmsg[tp]
    for k in range(N - 1):
        total = total + grcv[k]
    by_example(gmat, jnp.concatenate([total[0:4, :], total[4:8, :]], axis=1))
    t1 = dot_nt(gmat[...], iph2(), HIGHEST)
    _, lane = iota2((16, 128))
    both = jnp.where(((lane >> 2) & 1) == 0, t1, t2[...])
    row, col = iota2((128, 128))
    feature = ((row >> 3) << 2) + (row & 3)
    wanted = ((col >> 3) << 1) + (col & 1)
    erow, lane = iota2((16, 128))
    for half in range(2):
        place = jnp.where(feature == wanted + 32 * half, 1.0, 0.0)
        moved = dot(both, place, HIGHEST)
        moved = jnp.where((erow >> 2) == ((lane >> 1) & 3), moved, 0.0)
        pall[dp, 4 * half : 4 * half + 4, :] = (
            moved[0:4, :] + moved[4:8, :] + moved[8:12, :] + moved[12:16, :]
        )
    exchange(4, lambda peer: pall.at[dp], lambda k: pall.at[dp], "dp")
    exchanged(4, pall.at[pl.ds(0, N - 1)])
    sketch = pall[...].reshape(128, 128)
    hi, lo = split(sketch)
    squares = dot_nt(jnp.ones((8, 128), jnp.float32), sketch * sketch, HIGHEST)
    r = []
    for jh in range(2):
        qq = qj[:, :, 128 * jh : 128 * jh + 128].reshape(N * 32, 128)
        r.append(dot_nt(qq, hi) + dot_nt(qq, lo))
    _, lane = iota2((N * 32, 128))
    part = jnp.where(((lane >> 2) & 1) == 0, r[0], r[1])
    scm[:, 0:32, :] = part.reshape(N, 32, 128)
    scm[:, 32:40, :] = jnp.broadcast_to(squares[None], (N, 8, 128))
    exchange(5, lambda peer: scm.at[peer], lambda k: scr.at[k - 1], "tp")
    exchanged(5, scr)
    total = scm[tp]
    for k in range(N - 1):
        total = total + scr[k]
    row, col = iota2((64, 128))
    pick = jnp.where(((row >> 2) == (col >> 3)) & ((row & 3) == (col & 3)), 1.0, 0.0)
    full = dot_nt(total, pick, HIGHEST)
    scale = lax.rsqrt(full[32:33, :] * (1.0 / 4096.0) + 1e-06) * (1.0 / 64.0)
    out_ref[...] = full[0:32, :] * scale


def local(
    inputs, gate_pre, up_pre, out_grads, down_weight, example_ids,
    input_factor, gate_factor, up_factor, hidden_factor, output_factor, queries,
):
    hbm = pl.BlockSpec(memory_space=pl.ANY)
    vmem = pl.BlockSpec(memory_space=pltpu.VMEM)
    bf16, f32 = jnp.bfloat16, jnp.float32
    dma = pltpu.SemaphoreType.DMA
    return pl.pallas_call(
        kernel,
        out_shape=jax.ShapeDtypeStruct((32, 64), f32),
        in_specs=[hbm, hbm, hbm, hbm, hbm, vmem, vmem, vmem, vmem, vmem, hbm, hbm],
        out_specs=vmem,
        scratch_shapes=[
            pltpu.VMEM((N, TOK, DS), bf16),
            pltpu.VMEM((N, FS, DS), bf16),
            pltpu.VMEM((TOK, DS), bf16),
            pltpu.VMEM((TOK, FS), bf16),
            pltpu.VMEM((TOK, FS), bf16),
            pltpu.VMEM((64, N * DS), bf16),
            pltpu.VMEM((32, 4096), bf16),
            pltpu.VMEM((N, 256, 128), f32),
            pltpu.VMEM((N, 32, 256), bf16),
            pltpu.VMEM((NCH, TOK, 2 * CH), f32),
            pltpu.VMEM((2, NCH, 128, 2 * CH), bf16),
            pltpu.VMEM((TOK, 128), f32),
            pltpu.VMEM((TOK, 2 * CH), f32),
            pltpu.VMEM((N, 8, TOK), f32),
            pltpu.VMEM((N - 1, 8, TOK), f32),
            pltpu.VMEM((N, 8, TOK), f32),
            pltpu.VMEM((N, 8, TOK), f32),
            pltpu.VMEM((16, TOK), f32),
            pltpu.VMEM((16, TOK), f32),
            pltpu.VMEM((16, 128), f32),
            pltpu.VMEM((TOK // 2, 128), f32),
            pltpu.VMEM((N, 8, TOK // 2), f32),
            pltpu.VMEM((N - 1, 8, TOK // 2), f32),
            pltpu.VMEM((N, 8, 128), f32),
            pltpu.VMEM((N, 32, 256), bf16),
            pltpu.VMEM((N, 40, 128), f32),
            pltpu.VMEM((N - 1, 40, 128), f32),
            dma((7,)),
            dma((4 * NCH,)),
            dma((4 * NCH,)),
            dma((16 * NCH,)),
            dma((16 * NCH,)),
            dma,
            dma,
            dma((8,)),
            dma((8,)),
            dma((8,)),
            dma((8,)),
            dma((6,)),
            dma((6,)),
        ],
        compiler_params=pltpu.CompilerParams(
            collective_id=0, has_side_effects=True, vmem_limit_bytes=60 * 1024 * 1024
        ),
        cost_estimate=pl.CostEstimate(
            flops=2 * TOK * FS * N * DS, bytes_accessed=8 * 1024 * 1024, transcendentals=TOK * FS
        ),
        name="gather_and_score",
    )(
        inputs, gate_pre, up_pre, out_grads, down_weight, example_ids,
        input_factor.T, gate_factor.T, up_factor.T, hidden_factor.T, output_factor.T, queries,
    ).T


def solution(mesh):
    return jax.shard_map(
        local,
        mesh=mesh,
        in_specs=(
            P("dp", "tp"),
            P("dp", "tp"),
            P("dp", "tp"),
            P("dp", "tp"),
            P("tp", "dp"),
            P("dp"),
            P("tp", None),
            P("tp", None),
            P("tp", None),
            P("tp", None),
            P(),
            P(("dp", "tp"), None),
        ),
        out_specs=P(None, ("dp", "tp")),
        check_vma=False,
    )
```

```python
import functools

import jax
import jax.numpy as jnp
from jax import lax
from jax.experimental import pallas as pl
from jax.experimental.pallas import tpu as pltpu
from jax.sharding import PartitionSpec as P

TOK = 768
DS = 512
FS = 896
CH = 128
NCH = FS // CH
YF = NCH - 1
YR = 96
START = (0, 128, 256, 384, 512, 768, 768 - YR)
LENGTH = (128, 128, 128, 128, 256 - YR, 128, YR)
N = 16
MESH = pl.DeviceIdType.MESH
HIGHEST = lax.Precision.HIGHEST
NT = (((1,), (1,)), ((), ()))


def dot(a, b, precision=None):
    return jnp.dot(a, b, preferred_element_type=jnp.float32, precision=precision)


def dot_nt(a, b, precision=None):
    return lax.dot_general(a, b, NT, preferred_element_type=jnp.float32, precision=precision)


def split(x):
    hi = x.astype(jnp.bfloat16)
    lo = (x - hi.astype(jnp.float32)).astype(jnp.bfloat16)
    return hi, lo


def iota2(shape):
    return (
        lax.broadcasted_iota(jnp.int32, shape, 0),
        lax.broadcasted_iota(jnp.int32, shape, 1),
    )


def spread(kind):
    row, col = iota2((128, 64))
    hit = (col == ((row >> 3) << 2) + (row & 3)) & (((row >> 2) & 1) == kind)
    return jnp.where(hit, 1.0, 0.0).astype(jnp.bfloat16)


def kernel(
    in_hbm, gate_hbm, up_hbm, og_hbm, w_hbm, ids_ref, inf_ref, gf_ref, uf_ref, hf_ref, of_hbm, q_hbm,
    out_ref,
    ogb, wb, inb, gb, ub, ofb, qn, qt, qb, ab, fp, acc, acc2, pih_msg, pih_rcv, iph, opt, gmat, omat, t2,
    gacc, gmsg, grcv, pall, qj, scm, scr,
    loc_sem, zs_s, zs_r, ys_s, ys_r, oz_s, oz_r, ox_s, ox_r, oc_s, oc_r, small_s, small_r,
):
    dp, tp = lax.axis_index("dp"), lax.axis_index("tp")
    x, zl, core = tp >> 2, (tp >> 1) & 1, tp & 1
    y, zh = dp >> 2, dp & 3

    def dev(d, t):
        return {"dp": d, "tp": t}

    def remote(src, dst, ss, rs, d, t):
        return pltpu.make_async_remote_copy(
            src_ref=src, dst_ref=dst, send_sem=ss, recv_sem=rs,
            device_id=dev(d, t), device_id_type=MESH,
        )

    pending = []

    def send(src, dst, ss, rs, d, t):
        copy = remote(src, dst, ss, rs, d, t)
        copy.start()
        pending.append(copy)

    def arrived(dst, rs):
        remote(dst, dst, rs, rs, dp, tp ^ 1).wait_recv()

    loads = []
    for n, (src, dst) in enumerate((
        (w_hbm, wb.at[dp]), (og_hbm, ogb.at[tp]), (in_hbm, inb), (gate_hbm, gb), (up_hbm, ub),
        (q_hbm, qn), (of_hbm, ofb),
    )):
        copy = pltpu.make_async_copy(src, dst, loc_sem.at[n])
        copy.start()
        loads.append(copy)
    barrier = pltpu.get_barrier_semaphore()
    for k in range(1, N):
        pl.semaphore_signal(barrier, 1, device_id=dev(dp, tp ^ k), device_id_type=MESH)
        pl.semaphore_signal(barrier, 1, device_id=dev(dp ^ k, tp), device_id_type=MESH)
    pl.semaphore_wait(barrier, 2 * (N - 1))
    loads[0].wait()
    loads[1].wait()

    zh_up, zh_down = (zh + 1) & 3, (zh + 3) & 3
    y_up, y_down = (y + 1) & 3, (y + 3) & 3
    zh_of = (zh, zh_down, zh_up, (zh + 2) & 3)

    def at(yy, zz):
        return yy * 4 + zz

    def rows(i, part=None):
        if part is None:
            return pl.ds(START[i], LENGTH[i])
        return pl.ds(START[i] + part * (LENGTH[i] // 2), LENGTH[i] // 2)

    def w_send(block, r, sems, idx, target):
        ss, rs = sems
        ref = wb.at[block, r]
        remote(ref, ref, ss, rs.at[idx], target, tp).start()

    def z_own(i):
        w_send(dp, rows(i), (zs_s, zs_r), 4 * i, at(y, zh_up))
        w_send(dp, rows(i), (zs_s, zs_r), 4 * i + 1, at(y, zh_down))

    def z_forward(i):
        arrived(wb.at[at(y, zh_down), rows(i)], zs_r.at[4 * i])
        w_send(at(y, zh_down), rows(i, 0), (zs_s, zs_r), 4 * i + 2, at(y, zh_up))
        arrived(wb.at[at(y, zh_up), rows(i)], zs_r.at[4 * i + 1])
        w_send(at(y, zh_up), rows(i, 1), (zs_s, zs_r), 4 * i + 3, at(y, zh_down))

    def z_last(i):
        for part in range(2):
            arrived(wb.at[at(y, zh_of[3]), rows(i, part)], zs_r.at[4 * i + 2 + part])

    def y_send(i, q):
        base = 16 * i + 4 * q
        w_send(at(y, zh_of[q]), rows(i), (ys_s, ys_r), base, at(y_up, zh))
        w_send(at(y, zh_of[q]), rows(i), (ys_s, ys_r), base + 1, at(y_down, zh))

    def y_forward(i, q):
        base = 16 * i + 4 * q
        arrived(wb.at[at(y_down, zh_of[q]), rows(i)], ys_r.at[base])
        w_send(at(y_down, zh_of[q]), rows(i, 0), (ys_s, ys_r), base + 2, at(y_up, zh))
        arrived(wb.at[at(y_up, zh_of[q]), rows(i)], ys_r.at[base + 1])
        w_send(at(y_up, zh_of[q]), rows(i, 1), (ys_s, ys_r), base + 3, at(y_down, zh))

    def y_last(i, q):
        base = 16 * i + 4 * q
        for part in range(2):
            arrived(wb.at[at((y + 2) & 3, zh_of[q]), rows(i, part)], ys_r.at[base + 2 + part])

    y_of = (y, y_down, y_up, (y + 2) & 3)

    def yo_send():
        w_send(dp, rows(YF), (zs_s, zs_r), 4 * YF, at(y_up, zh))
        w_send(dp, rows(YF), (zs_s, zs_r), 4 * YF + 1, at(y_down, zh))

    def yo_forward():
        arrived(wb.at[at(y_down, zh), rows(YF)], zs_r.at[4 * YF])
        w_send(at(y_down, zh), rows(YF, 0), (zs_s, zs_r), 4 * YF + 2, at(y_up, zh))
        arrived(wb.at[at(y_up, zh), rows(YF)], zs_r.at[4 * YF + 1])
        w_send(at(y_up, zh), rows(YF, 1), (zs_s, zs_r), 4 * YF + 3, at(y_down, zh))

    def yo_last():
        for part in range(2):
            arrived(wb.at[at(y_of[3], zh), rows(YF, part)], zs_r.at[4 * YF + 2 + part])

    def zq_send(q):
        base = 16 * YF + 4 * q
        w_send(at(y_of[q], zh), rows(YF), (ys_s, ys_r), base, at(y, zh_up))
        w_send(at(y_of[q], zh), rows(YF), (ys_s, ys_r), base + 1, at(y, zh_down))

    def zq_forward(q):
        base = 16 * YF + 4 * q
        arrived(wb.at[at(y_of[q], zh_down), rows(YF)], ys_r.at[base])
        w_send(at(y_of[q], zh_down), rows(YF, 0), (ys_s, ys_r), base + 2, at(y, zh_up))
        arrived(wb.at[at(y_of[q], zh_up), rows(YF)], ys_r.at[base + 1])
        w_send(at(y_of[q], zh_up), rows(YF, 1), (ys_s, ys_r), base + 3, at(y, zh_down))

    def zq_last(q):
        base = 16 * YF + 4 * q
        for part in range(2):
            arrived(wb.at[at(y_of[q], zh_of[3]), rows(YF, part)], ys_r.at[base + 2 + part])

    x_up, x_down, x_far = (x + 1) & 3, (x + 3) & 3, (x + 2) & 3

    def tat(xx, zz, cc):
        return xx * 4 + zz * 2 + cc

    zl_of = (zl, 1 - zl)

    def o_core(slot, idx):
        send(ogb.at[slot], ogb.at[slot], oc_s.at[idx], oc_r.at[idx], dp, tp ^ 1)

    def o_x(q):
        slot = tat(x, zl_of[q], core)
        send(ogb.at[slot], ogb.at[slot], ox_s.at[4 * q], ox_r.at[4 * q], dp, tat(x_up, zl, core))
        send(ogb.at[slot], ogb.at[slot], ox_s.at[4 * q + 1], ox_r.at[4 * q + 1], dp, tat(x_down, zl, core))

    def o_part(slot, part):
        return ogb.at[slot, pl.ds(part * (TOK // 2), TOK // 2)]

    def o_forward(q):
        slot = tat(x_down, zl_of[q], core)
        arrived(ogb.at[slot], ox_r.at[4 * q])
        ref = o_part(slot, 0)
        send(ref, ref, ox_s.at[4 * q + 2], ox_r.at[4 * q + 2], dp, tat(x_up, zl, core))
        o_core(slot, 2 + 3 * q)
        slot = tat(x_up, zl_of[q], core)
        arrived(ogb.at[slot], ox_r.at[4 * q + 1])
        ref = o_part(slot, 1)
        send(ref, ref, ox_s.at[4 * q + 3], ox_r.at[4 * q + 3], dp, tat(x_down, zl, core))
        o_core(slot, 3 + 3 * q)

    def o_last(q):
        slot = tat(x_far, zl_of[q], core)
        for part in range(2):
            arrived(o_part(slot, part), ox_r.at[4 * q + 2 + part])
        o_core(slot, 4 + 3 * q)

    def o_all():
        other = 1 - core
        arrived(ogb.at[tat(x, zl, other)], oc_r.at[0])
        arrived(ogb.at[tat(x, 1 - zl, other)], oc_r.at[1])
        for q in range(2):
            for k, xx in enumerate((x_down, x_up, x_far)):
                arrived(ogb.at[tat(xx, zl_of[q], other)], oc_r.at[2 + 3 * q + k])

    def exchange(idx, src_of, dst_of, axis):
        for k in (8, 9, 10, 11, 12, 13, 14, 15, 4, 5, 6, 7, 2, 3, 1):
            d, t = (dp ^ k, tp) if axis == "dp" else (dp, tp ^ k)
            peer = d if axis == "dp" else t
            remote(src_of(peer), dst_of(k), small_s.at[idx], small_r.at[idx], d, t).start()

    def exchanged(idx, fifteen):
        copy = remote(fifteen, fifteen, small_s.at[idx], small_r.at[idx], dp, tp ^ 1)
        copy.wait_recv()
        copy.wait_send()

    z_own(0)
    send(ogb.at[tp], ogb.at[tp], oz_s, oz_r, dp, tat(x, 1 - zl, core))
    o_x(0)
    y_send(0, 0)
    yo_send()
    o_core(tp, 0)
    z_own(1)
    for i in range(1, YF):
        y_send(i, 0)

    def early():
        for n in range(2, 5):
            loads[n].wait()
        sel0, sel1 = spread(0), spread(1)
        acc[...] = dot_nt(inb[...], dot(sel0, inf_ref[...]).astype(jnp.bfloat16))

        @pl.loop(0, NCH)
        def _(i):
            lanes = pl.ds(pl.multiple_of(i * CH, CH), CH)
            g = gb[:, lanes].astype(jnp.float32)
            u = ub[:, lanes].astype(jnp.float32)
            s = jax.nn.sigmoid(g)
            activated = g * s
            ab[i, :, :CH] = u * s * (1.0 + g * (1.0 - s))
            ab[i, :, CH:] = activated
            hi, lo = split(activated * u)
            hfp = dot(sel1, hf_ref[:, lanes]).astype(jnp.bfloat16)
            acc[...] += dot_nt(hi, hfp) + dot_nt(lo, hfp)
            for h, sel in enumerate((sel0, sel1)):
                fp[h, i, :, :CH] = dot(sel, gf_ref[:, lanes]).astype(jnp.bfloat16)
                fp[h, i, :, CH:] = dot(sel, uf_ref[:, lanes]).astype(jnp.bfloat16)

        pih_msg[...] = acc[...].T.reshape(N, 8, TOK)
        exchange(0, lambda peer: pih_msg.at[peer], lambda k: pih_rcv.at[k - 1], "tp")

    def spread_queries():
        loads[5].wait()
        row, col = iota2((128, 128))
        hit = col == ((row & 1) << 6) + ((row >> 3) << 2) + ((row >> 1) & 3)
        place = jnp.where(hit, 1.0, 0.0).astype(jnp.bfloat16)
        for m in range(32):
            moved = dot_nt(place, qn[:, 128 * m : 128 * m + 128])
            qt[:, 8 * m : 8 * m + 8, 0:32] = moved.reshape(N, 8, 32)

        @pl.loop(0, N)
        def _(k):
            for half in range(2):
                turned = qt[k, 128 * half : 128 * half + 128, :].T
                qb[k, :, 128 * half : 128 * half + 128] = turned[0:32, :].astype(jnp.bfloat16)

        exchange(1, lambda peer: qb.at[peer], lambda k: qj.at[tp], "tp")

    def middle():
        exchanged(0, pih_rcv)
        total = pih_msg[tp]
        for k in range(N - 1):
            total = total + pih_rcv[k]
        iph[tp] = total
        exchange(2, lambda peer: iph.at[tp], lambda k: iph.at[tp], "tp")

    def mask():
        row, _ = iota2((4, TOK))
        return jnp.where(ids_ref[...].reshape(1, TOK) == dp * 4 + row, 1.0, 0.0)

    def by_example(dst, cols):
        m = mask()
        for jj in range(4):
            dst[4 * jj : 4 * jj + 4, :] = m * cols[jj : jj + 1, :]

    def iph2():
        return iph[...].reshape(N * 8, TOK)

    def output_side():
        loads[6].wait()
        sel0 = spread(0)
        acc[...] = jnp.zeros_like(acc)

        @pl.loop(0, N)
        def _(k):
            ofp = dot(sel0, ofb[:, pl.ds(pl.multiple_of(k * DS, DS), DS)]).astype(jnp.bfloat16)
            acc[...] += dot_nt(ogb[k], ofp)

        opt[...] = acc[...].T.reshape(N, 8, TOK)
        by_example(omat, opt[tp])
        exchanged(2, iph.at[pl.ds(0, N - 1)])
        t2[...] = dot_nt(omat[...], iph2(), HIGHEST)
        exchanged(1, qj.at[pl.ds(0, N - 1)])
        qj[tp] = qb[tp]
        gacc[...] = jnp.zeros_like(gacc)

    def multiply(out, place, width, ks, first):
        if first:
            out[...] = jnp.zeros_like(out)

        @pl.loop(0, 4)
        def _(n):
            for k in ks:
                slot = k(n)
                out[...] += dot_nt(ogb[slot], wb[slot, pl.ds(place * CH, width * CH), :])

    def project(source, place, half):
        for h in range(2):
            tok = slice(h * (TOK // 2), (h + 1) * (TOK // 2))
            c = source[tok, half * CH : half * CH + CH]
            hi, lo = split(jnp.concatenate([c * ab[place, tok, :CH], c * ab[place, tok, CH:]], axis=1))
            gacc[...] += dot_nt(hi, fp[h, place]) + dot_nt(lo, fp[h, place])

    def slot_of(q):
        return lambda n: n * 4 + zh_of[q]

    every = [slot_of(q) for q in range(4)]

    def compute_pair(place):
        multiply(acc2, place, 2, every, True)
        project(acc2, place, 0)
        project(acc2, place + 1, 1)

    def y_wait(i, qs):
        for q in qs:
            y_last(i, q)

    early()
    for i in range(YF + 2):
        if i < YF:
            z_forward(i)
            y_send(i, 1)
            y_send(i, 2)
            if i + 2 < YF:
                z_own(i + 2)
        if 1 <= i <= YF:
            z_last(i - 1)
            y_send(i - 1, 3)
        if i == 0:
            yo_forward()
            for k in range(YF):
                y_forward(k, 0)
            o_forward(0)
        if 1 <= i <= YF:
            y_forward(i - 1, 1)
            y_forward(i - 1, 2)
        if 2 <= i <= YF + 1:
            y_forward(i - 2, 3)
        if i == 1:
            slot = tat(x, 1 - zl, core)
            arrived(ogb.at[slot], oz_r)
            o_x(1)
            o_core(slot, 1)
            middle()
            spread_queries()
        if i == 3:
            o_forward(1)
            o_last(0)
        if i == 4:
            yo_last()
            for q in range(4):
                zq_send(q)
            o_last(1)
            o_all()
            output_side()
            y_wait(0, range(4))
            y_wait(1, range(4))
            compute_pair(0)
        if i == 5:
            for q in range(4):
                zq_forward(q)
            y_wait(2, range(4))
            y_wait(3, range(3))
            multiply(acc2, 2, 2, every[:3], True)
        if i == 6:
            y_wait(3, [3])
            multiply(acc2, 2, 2, every[3:], False)
            project(acc2, 2, 0)
            project(acc2, 3, 1)
            y_wait(4, range(3))
            multiply(acc2, 4, 2, every[:3], True)
    y_wait(5, range(3))
    multiply(acc, 6, 1, every[:3], True)
    y_wait(4, [3])
    for q in range(4):
        zq_last(q)
    multiply(acc2, 4, 2, every[3:], False)
    project(acc2, 4, 0)
    project(acc2, 5, 1)
    y_wait(5, [3])
    multiply(acc, 6, 1, every[3:], False)
    project(acc, 6, 0)

    gmsg[...] = gacc[...].T.reshape(N, 8, TOK // 2)
    exchange(3, lambda peer: gmsg.at[peer], lambda k: grcv.at[k - 1], "tp")
    for copy in pending:
        copy.wait_send()
    for sem, blocks in ((zs_s, 3), (ys_s, 12)):
        ref = wb.at[pl.ds(0, blocks)]
        remote(ref, ref, sem, sem, dp, tp ^ 1).wait_send()
    exchanged(3, grcv)
    total = gmsg[tp]
    for k in range(N - 1):
        total = total + grcv[k]
    by_example(gmat, jnp.concatenate([total[0:4, :], total[4:8, :]], axis=1))
    t1 = dot_nt(gmat[...], iph2(), HIGHEST)
    _, lane = iota2((16, 128))
    both = jnp.where(((lane >> 2) & 1) == 0, t1, t2[...])
    row, col = iota2((128, 128))
    feature = ((row >> 3) << 2) + (row & 3)
    wanted = ((col >> 3) << 1) + (col & 1)
    erow, lane = iota2((16, 128))
    for half in range(2):
        place = jnp.where(feature == wanted + 32 * half, 1.0, 0.0)
        moved = dot(both, place, HIGHEST)
        moved = jnp.where((erow >> 2) == ((lane >> 1) & 3), moved, 0.0)
        pall[dp, 4 * half : 4 * half + 4, :] = (
            moved[0:4, :] + moved[4:8, :] + moved[8:12, :] + moved[12:16, :]
        )
    exchange(4, lambda peer: pall.at[dp], lambda k: pall.at[dp], "dp")
    exchanged(4, pall.at[pl.ds(0, N - 1)])
    sketch = pall[...].reshape(128, 128)
    hi, lo = split(sketch)
    squares = dot_nt(jnp.ones((8, 128), jnp.float32), sketch * sketch, HIGHEST)
    r = []
    for jh in range(2):
        qq = qj[:, :, 128 * jh : 128 * jh + 128].reshape(N * 32, 128)
        r.append(dot_nt(qq, hi) + dot_nt(qq, lo))
    _, lane = iota2((N * 32, 128))
    part = jnp.where(((lane >> 2) & 1) == 0, r[0], r[1])
    down = (part + pltpu.roll(part, 124, 1)).reshape(N, 32, 128)
    up = (part + pltpu.roll(part, 4, 1)).reshape(N, 32, 128)
    _, lane = iota2((16, 128))
    scm[:, 0:16, :] = jnp.where((((lane >> 2) & 1) == 0)[None], down[:, 0:16, :], up[:, 16:32, :])
    scm[:, 16:24, :] = jnp.broadcast_to(squares[None], (N, 8, 128))
    exchange(5, lambda peer: scm.at[peer], lambda k: scr.at[k - 1], "tp")
    exchanged(5, scr)
    total = scm[tp]
    for k in range(N - 1):
        total = total + scr[k]
    row, col = iota2((64, 128))
    pick = jnp.where(((row >> 2) == (col >> 3)) & ((row & 3) == (col & 3)), 1.0, 0.0)
    square = dot_nt(total[16:24, :], pick, HIGHEST)[0:1, :]
    scale = lax.rsqrt(square * (1.0 / 4096.0) + 1e-06) * (1.0 / 64.0)
    for half in range(2):
        here = jnp.where(((col >> 2) & 1) == half, pick, 0.0)
        out_ref[16 * half : 16 * half + 16, :] = dot_nt(total[0:16, :], here, HIGHEST) * scale


def local(
    inputs, gate_pre, up_pre, out_grads, down_weight, example_ids,
    input_factor, gate_factor, up_factor, hidden_factor, output_factor, queries,
):
    hbm = pl.BlockSpec(memory_space=pl.ANY)
    vmem = pl.BlockSpec(memory_space=pltpu.VMEM)
    bf16, f32 = jnp.bfloat16, jnp.float32
    dma = pltpu.SemaphoreType.DMA
    return pl.pallas_call(
        kernel,
        out_shape=jax.ShapeDtypeStruct((32, 64), f32),
        in_specs=[hbm, hbm, hbm, hbm, hbm, vmem, vmem, vmem, vmem, vmem, hbm, hbm],
        out_specs=vmem,
        scratch_shapes=[
            pltpu.VMEM((N, TOK, DS), bf16),
            pltpu.VMEM((N, FS, DS), bf16),
            pltpu.VMEM((TOK, DS), bf16),
            pltpu.VMEM((TOK, FS), bf16),
            pltpu.VMEM((TOK, FS), bf16),
            pltpu.VMEM((64, N * DS), bf16),
            pltpu.VMEM((32, 4096), bf16),
            pltpu.VMEM((N, 256, 128), f32),
            pltpu.VMEM((N, 32, 256), bf16),
            pltpu.VMEM((NCH, TOK, 2 * CH), f32),
            pltpu.VMEM((2, NCH, 128, 2 * CH), bf16),
            pltpu.VMEM((TOK, 128), f32),
            pltpu.VMEM((TOK, 2 * CH), f32),
            pltpu.VMEM((N, 8, TOK), f32),
            pltpu.VMEM((N - 1, 8, TOK), f32),
            pltpu.VMEM((N, 8, TOK), f32),
            pltpu.VMEM((N, 8, TOK), f32),
            pltpu.VMEM((16, TOK), f32),
            pltpu.VMEM((16, TOK), f32),
            pltpu.VMEM((16, 128), f32),
            pltpu.VMEM((TOK // 2, 128), f32),
            pltpu.VMEM((N, 8, TOK // 2), f32),
            pltpu.VMEM((N - 1, 8, TOK // 2), f32),
            pltpu.VMEM((N, 8, 128), f32),
            pltpu.VMEM((N, 32, 256), bf16),
            pltpu.VMEM((N, 24, 128), f32),
            pltpu.VMEM((N - 1, 24, 128), f32),
            dma((7,)),
            dma,
            dma((4 * NCH,)),
            dma,
            dma((16 * NCH,)),
            dma,
            dma,
            dma((8,)),
            dma((8,)),
            dma((8,)),
            dma((8,)),
            dma((6,)),
            dma((6,)),
        ],
        compiler_params=pltpu.CompilerParams(
            collective_id=0, has_side_effects=True, vmem_limit_bytes=60 * 1024 * 1024
        ),
        cost_estimate=pl.CostEstimate(
            flops=2 * TOK * FS * N * DS, bytes_accessed=8 * 1024 * 1024, transcendentals=TOK * FS
        ),
        name="gather_and_score",
    )(
        inputs, gate_pre, up_pre, out_grads, down_weight, example_ids,
        input_factor.T, gate_factor.T, up_factor.T, hidden_factor.T, output_factor.T, queries,
    ).T


def solution(mesh):
    return jax.shard_map(
        local,
        mesh=mesh,
        in_specs=(
            P("dp", "tp"),
            P("dp", "tp"),
            P("dp", "tp"),
            P("dp", "tp"),
            P("tp", "dp"),
            P("dp"),
            P("tp", None),
            P("tp", None),
            P("tp", None),
            P("tp", None),
            P(),
            P(("dp", "tp"), None),
        ),
        out_specs=P(None, ("dp", "tp")),
        check_vma=False,
    )
```

```python
import functools

import jax
import jax.numpy as jnp
from jax import lax
from jax.experimental import pallas as pl
from jax.experimental.pallas import tpu as pltpu
from jax.sharding import PartitionSpec as P

TOK = 768
DS = 512
FS = 896
CH = 128
NCH = FS // CH
YF = NCH - 1
YR = 96
START = (0, 128, 256, 384, 512, 768, 768 - YR)
LENGTH = (128, 128, 128, 128, 256 - YR, 128, YR)
N = 16
MESH = pl.DeviceIdType.MESH
HIGHEST = lax.Precision.HIGHEST
NT = (((1,), (1,)), ((), ()))


def dot(a, b, precision=None):
    return jnp.dot(a, b, preferred_element_type=jnp.float32, precision=precision)


def dot_nt(a, b, precision=None):
    return lax.dot_general(a, b, NT, preferred_element_type=jnp.float32, precision=precision)


def split(x):
    hi = x.astype(jnp.bfloat16)
    lo = (x - hi.astype(jnp.float32)).astype(jnp.bfloat16)
    return hi, lo


def iota2(shape):
    return (
        lax.broadcasted_iota(jnp.int32, shape, 0),
        lax.broadcasted_iota(jnp.int32, shape, 1),
    )


def spread(kind):
    row, col = iota2((128, 64))
    hit = (col == ((row >> 3) << 2) + (row & 3)) & (((row >> 2) & 1) == kind)
    return jnp.where(hit, 1.0, 0.0).astype(jnp.bfloat16)


def kernel(
    in_hbm, gate_hbm, up_hbm, og_hbm, w_hbm, ids_ref, inf_ref, gf_ref, uf_ref, hf_ref, of_hbm, q_hbm,
    out_ref,
    ogb, wb, inb, gb, ub, ofb, qn, qt, qb, ab, fp, acc, acc2, pih_msg, pih_rcv, iph, opt, gmat, omat, t2,
    gacc, gmsg, grcv, pall, qj, scm, scr,
    loc_sem, zs_s, zs_r, ys_s, ys_r, oz_s, oz_r, ox_s, ox_r, oc_s, oc_r, small_s, small_r,
):
    dp, tp = lax.axis_index("dp"), lax.axis_index("tp")
    x, zl, core = tp >> 2, (tp >> 1) & 1, tp & 1
    y, zh = dp >> 2, dp & 3

    def dev(d, t):
        return {"dp": d, "tp": t}

    def remote(src, dst, ss, rs, d, t):
        return pltpu.make_async_remote_copy(
            src_ref=src, dst_ref=dst, send_sem=ss, recv_sem=rs,
            device_id=dev(d, t), device_id_type=MESH,
        )

    pending = []

    def send(src, dst, ss, rs, d, t):
        copy = remote(src, dst, ss, rs, d, t)
        copy.start()
        pending.append(copy)

    def arrived(dst, rs):
        remote(dst, dst, rs, rs, dp, tp ^ 1).wait_recv()

    loads = []
    for n, (src, dst) in enumerate((
        (w_hbm, wb.at[dp]), (og_hbm, ogb.at[tp]), (in_hbm, inb), (gate_hbm, gb), (up_hbm, ub),
        (q_hbm, qn), (of_hbm, ofb),
    )):
        copy = pltpu.make_async_copy(src, dst, loc_sem.at[n])
        copy.start()
        loads.append(copy)
    barrier = pltpu.get_barrier_semaphore()
    for k in range(1, N):
        pl.semaphore_signal(barrier, 1, device_id=dev(dp, tp ^ k), device_id_type=MESH)
        pl.semaphore_signal(barrier, 1, device_id=dev(dp ^ k, tp), device_id_type=MESH)
    pl.semaphore_wait(barrier, 2 * (N - 1))
    loads[0].wait()
    loads[1].wait()

    zh_up, zh_down = (zh + 1) & 3, (zh + 3) & 3
    y_up, y_down = (y + 1) & 3, (y + 3) & 3
    zh_of = (zh, zh_down, zh_up, (zh + 2) & 3)

    def at(yy, zz):
        return yy * 4 + zz

    def rows(i, part=None):
        if part is None:
            return pl.ds(START[i], LENGTH[i])
        return pl.ds(START[i] + part * (LENGTH[i] // 2), LENGTH[i] // 2)

    def w_send(block, r, sems, idx, target):
        ss, rs = sems
        ref = wb.at[block, r]
        remote(ref, ref, ss, rs.at[idx], target, tp).start()

    def z_own(i):
        w_send(dp, rows(i), (zs_s, zs_r), 4 * i, at(y, zh_up))
        w_send(dp, rows(i), (zs_s, zs_r), 4 * i + 1, at(y, zh_down))

    def z_forward(i):
        arrived(wb.at[at(y, zh_down), rows(i)], zs_r.at[4 * i])
        w_send(at(y, zh_down), rows(i, 0), (zs_s, zs_r), 4 * i + 2, at(y, zh_up))
        arrived(wb.at[at(y, zh_up), rows(i)], zs_r.at[4 * i + 1])
        w_send(at(y, zh_up), rows(i, 1), (zs_s, zs_r), 4 * i + 3, at(y, zh_down))

    def z_last(i):
        for part in range(2):
            arrived(wb.at[at(y, zh_of[3]), rows(i, part)], zs_r.at[4 * i + 2 + part])

    def y_send(i, q):
        base = 16 * i + 4 * q
        w_send(at(y, zh_of[q]), rows(i), (ys_s, ys_r), base, at(y_up, zh))
        w_send(at(y, zh_of[q]), rows(i), (ys_s, ys_r), base + 1, at(y_down, zh))

    def y_forward(i, q):
        base = 16 * i + 4 * q
        arrived(wb.at[at(y_down, zh_of[q]), rows(i)], ys_r.at[base])
        w_send(at(y_down, zh_of[q]), rows(i, 0), (ys_s, ys_r), base + 2, at(y_up, zh))
        arrived(wb.at[at(y_up, zh_of[q]), rows(i)], ys_r.at[base + 1])
        w_send(at(y_up, zh_of[q]), rows(i, 1), (ys_s, ys_r), base + 3, at(y_down, zh))

    def y_last(i, q):
        base = 16 * i + 4 * q
        for part in range(2):
            arrived(wb.at[at((y + 2) & 3, zh_of[q]), rows(i, part)], ys_r.at[base + 2 + part])

    y_of = (y, y_down, y_up, (y + 2) & 3)

    def yo_send():
        w_send(dp, rows(YF), (zs_s, zs_r), 4 * YF, at(y_up, zh))
        w_send(dp, rows(YF), (zs_s, zs_r), 4 * YF + 1, at(y_down, zh))

    def yo_forward():
        arrived(wb.at[at(y_down, zh), rows(YF)], zs_r.at[4 * YF])
        w_send(at(y_down, zh), rows(YF, 0), (zs_s, zs_r), 4 * YF + 2, at(y_up, zh))
        arrived(wb.at[at(y_up, zh), rows(YF)], zs_r.at[4 * YF + 1])
        w_send(at(y_up, zh), rows(YF, 1), (zs_s, zs_r), 4 * YF + 3, at(y_down, zh))

    def yo_last():
        for part in range(2):
            arrived(wb.at[at(y_of[3], zh), rows(YF, part)], zs_r.at[4 * YF + 2 + part])

    def zq_send(q):
        base = 16 * YF + 4 * q
        w_send(at(y_of[q], zh), rows(YF), (ys_s, ys_r), base, at(y, zh_up))
        w_send(at(y_of[q], zh), rows(YF), (ys_s, ys_r), base + 1, at(y, zh_down))

    def zq_forward(q):
        base = 16 * YF + 4 * q
        arrived(wb.at[at(y_of[q], zh_down), rows(YF)], ys_r.at[base])
        w_send(at(y_of[q], zh_down), rows(YF, 0), (ys_s, ys_r), base + 2, at(y, zh_up))
        arrived(wb.at[at(y_of[q], zh_up), rows(YF)], ys_r.at[base + 1])
        w_send(at(y_of[q], zh_up), rows(YF, 1), (ys_s, ys_r), base + 3, at(y, zh_down))

    def zq_last(q):
        base = 16 * YF + 4 * q
        for part in range(2):
            arrived(wb.at[at(y_of[q], zh_of[3]), rows(YF, part)], ys_r.at[base + 2 + part])

    x_up, x_down, x_far = (x + 1) & 3, (x + 3) & 3, (x + 2) & 3

    def tat(xx, zz, cc):
        return xx * 4 + zz * 2 + cc

    zl_of = (zl, 1 - zl)

    def o_core(slot, idx):
        send(ogb.at[slot], ogb.at[slot], oc_s.at[idx], oc_r.at[idx], dp, tp ^ 1)

    def o_x(q):
        slot = tat(x, zl_of[q], core)
        send(ogb.at[slot], ogb.at[slot], ox_s.at[4 * q], ox_r.at[4 * q], dp, tat(x_up, zl, core))
        send(ogb.at[slot], ogb.at[slot], ox_s.at[4 * q + 1], ox_r.at[4 * q + 1], dp, tat(x_down, zl, core))

    def o_part(slot, part):
        return ogb.at[slot, pl.ds(part * (TOK // 2), TOK // 2)]

    def o_forward(q):
        slot = tat(x_down, zl_of[q], core)
        arrived(ogb.at[slot], ox_r.at[4 * q])
        ref = o_part(slot, 0)
        send(ref, ref, ox_s.at[4 * q + 2], ox_r.at[4 * q + 2], dp, tat(x_up, zl, core))
        o_core(slot, 2 + 3 * q)
        slot = tat(x_up, zl_of[q], core)
        arrived(ogb.at[slot], ox_r.at[4 * q + 1])
        ref = o_part(slot, 1)
        send(ref, ref, ox_s.at[4 * q + 3], ox_r.at[4 * q + 3], dp, tat(x_down, zl, core))
        o_core(slot, 3 + 3 * q)

    def o_last(q):
        slot = tat(x_far, zl_of[q], core)
        for part in range(2):
            arrived(o_part(slot, part), ox_r.at[4 * q + 2 + part])
        o_core(slot, 4 + 3 * q)

    def o_all():
        other = 1 - core
        arrived(ogb.at[tat(x, zl, other)], oc_r.at[0])
        arrived(ogb.at[tat(x, 1 - zl, other)], oc_r.at[1])
        for q in range(2):
            for k, xx in enumerate((x_down, x_up, x_far)):
                arrived(ogb.at[tat(xx, zl_of[q], other)], oc_r.at[2 + 3 * q + k])

    def exchange(idx, src_of, dst_of, axis):
        for k in (8, 9, 10, 11, 12, 13, 14, 15, 4, 5, 6, 7, 2, 3, 1):
            d, t = (dp ^ k, tp) if axis == "dp" else (dp, tp ^ k)
            peer = d if axis == "dp" else t
            remote(src_of(peer), dst_of(k), small_s.at[idx], small_r.at[idx], d, t).start()

    def exchanged(idx, fifteen):
        copy = remote(fifteen, fifteen, small_s.at[idx], small_r.at[idx], dp, tp ^ 1)
        copy.wait_recv()
        copy.wait_send()

    z_own(0)
    send(ogb.at[tp], ogb.at[tp], oz_s, oz_r, dp, tat(x, 1 - zl, core))
    o_x(0)
    y_send(0, 0)
    yo_send()
    o_core(tp, 0)
    z_own(1)
    for i in range(1, YF):
        y_send(i, 0)

    def early():
        for n in range(2, 5):
            loads[n].wait()
        sel0, sel1 = spread(0), spread(1)
        acc[...] = dot_nt(inb[...], dot(sel0, inf_ref[...]).astype(jnp.bfloat16))

        @pl.loop(0, NCH)
        def _(i):
            lanes = pl.ds(pl.multiple_of(i * CH, CH), CH)
            g = gb[:, lanes].astype(jnp.float32)
            u = ub[:, lanes].astype(jnp.float32)
            s = jax.nn.sigmoid(g)
            activated = g * s
            ab[i, :, :CH] = u * s * (1.0 + g * (1.0 - s))
            ab[i, :, CH:] = activated
            hi, lo = split(activated * u)
            hfp = dot(sel1, hf_ref[:, lanes]).astype(jnp.bfloat16)
            acc[...] += dot_nt(hi, hfp) + dot_nt(lo, hfp)
            for h, sel in enumerate((sel0, sel1)):
                fp[h, i, :, :CH] = dot(sel, gf_ref[:, lanes]).astype(jnp.bfloat16)
                fp[h, i, :, CH:] = dot(sel, uf_ref[:, lanes]).astype(jnp.bfloat16)

        pih_msg[...] = acc[...].T.reshape(N, 8, TOK)
        exchange(0, lambda peer: pih_msg.at[peer], lambda k: pih_rcv.at[k - 1], "tp")

    def spread_queries():
        loads[5].wait()
        row, col = iota2((128, 128))
        hit = col == ((row & 1) << 6) + ((row >> 3) << 2) + ((row >> 1) & 3)
        place = jnp.where(hit, 1.0, 0.0).astype(jnp.bfloat16)
        for m in range(32):
            moved = dot_nt(place, qn[:, 128 * m : 128 * m + 128])
            qt[:, 8 * m : 8 * m + 8, 0:32] = moved.reshape(N, 8, 32)

        @pl.loop(0, N)
        def _(k):
            for half in range(2):
                turned = qt[k, 128 * half : 128 * half + 128, :].T
                qb[k, :, 128 * half : 128 * half + 128] = turned[0:32, :].astype(jnp.bfloat16)

        exchange(1, lambda peer: qb.at[peer], lambda k: qj.at[tp], "tp")

    def middle():
        exchanged(0, pih_rcv)
        total = pih_msg[tp]
        for k in range(N - 1):
            total = total + pih_rcv[k]
        iph[tp] = total
        exchange(2, lambda peer: iph.at[tp], lambda k: iph.at[tp], "tp")

    def mask():
        row, _ = iota2((4, TOK))
        return jnp.where(ids_ref[...].reshape(1, TOK) == dp * 4 + row, 1.0, 0.0)

    def by_example(dst, cols):
        m = mask()
        for jj in range(4):
            dst[4 * jj : 4 * jj + 4, :] = m * cols[jj : jj + 1, :]

    def iph2():
        return iph[...].reshape(N * 8, TOK)

    def output_side():
        loads[6].wait()
        sel0 = spread(0)
        acc[...] = jnp.zeros_like(acc)

        @pl.loop(0, N)
        def _(k):
            ofp = dot(sel0, ofb[:, pl.ds(pl.multiple_of(k * DS, DS), DS)]).astype(jnp.bfloat16)
            acc[...] += dot_nt(ogb[k], ofp)

        opt[...] = acc[...].T.reshape(N, 8, TOK)
        by_example(omat, opt[tp])
        exchanged(2, iph.at[pl.ds(0, N - 1)])
        t2[...] = dot_nt(omat[...], iph2(), HIGHEST)
        exchanged(1, qj.at[pl.ds(0, N - 1)])
        qj[tp] = qb[tp]
        gacc[...] = jnp.zeros_like(gacc)

    def multiply(out, place, width, ks, first):
        if first:
            out[...] = jnp.zeros_like(out)

        @pl.loop(0, 4)
        def _(n):
            for k in ks:
                slot = k(n)
                out[...] += dot_nt(ogb[slot], wb[slot, pl.ds(place * CH, width * CH), :])

    def project(source, place, half):
        for h in range(2):
            tok = slice(h * (TOK // 2), (h + 1) * (TOK // 2))
            c = source[tok, half * CH : half * CH + CH]
            hi, lo = split(jnp.concatenate([c * ab[place, tok, :CH], c * ab[place, tok, CH:]], axis=1))
            gacc[...] += dot_nt(hi, fp[h, place]) + dot_nt(lo, fp[h, place])

    def slot_of(q):
        return lambda n: n * 4 + zh_of[q]

    every = [slot_of(q) for q in range(4)]

    def compute_pair(place):
        multiply(acc2, place, 2, every, True)
        project(acc2, place, 0)
        project(acc2, place + 1, 1)

    def y_wait(i, qs):
        for q in qs:
            y_last(i, q)

    early()
    for i in range(YF + 2):
        if i < YF:
            z_forward(i)
            y_send(i, 1)
            y_send(i, 2)
            if i + 2 < YF:
                z_own(i + 2)
        if 1 <= i <= YF:
            z_last(i - 1)
            y_send(i - 1, 3)
        if i == 0:
            yo_forward()
            for k in range(YF):
                y_forward(k, 0)
            o_forward(0)
        if 1 <= i <= YF:
            y_forward(i - 1, 1)
            y_forward(i - 1, 2)
        if 2 <= i <= YF + 1:
            y_forward(i - 2, 3)
        if i == 1:
            slot = tat(x, 1 - zl, core)
            arrived(ogb.at[slot], oz_r)
            o_x(1)
            o_core(slot, 1)
            middle()
            spread_queries()
        if i == 3:
            o_forward(1)
            o_last(0)
        if i == 4:
            yo_last()
            for q in range(4):
                zq_send(q)
            o_last(1)
            o_all()
            output_side()
        if i == 5:
            for q in range(4):
                zq_forward(q)
            y_wait(0, range(4))
            y_wait(1, range(4))
            compute_pair(0)
            y_wait(2, range(4))
            y_wait(3, range(3))
            multiply(acc2, 2, 2, every[:3], True)
        if i == 6:
            y_wait(3, [3])
            multiply(acc2, 2, 2, every[3:], False)
            project(acc2, 2, 0)
            project(acc2, 3, 1)
            y_wait(4, range(3))
            multiply(acc2, 4, 2, every[:3], True)
    y_wait(5, range(3))
    multiply(acc, 6, 1, every[:3], True)
    y_wait(4, [3])
    for q in range(4):
        zq_last(q)
    multiply(acc2, 4, 2, every[3:], False)
    project(acc2, 4, 0)
    project(acc2, 5, 1)
    y_wait(5, [3])
    multiply(acc, 6, 1, every[3:], False)
    project(acc, 6, 0)

    gmsg[...] = gacc[...].T.reshape(N, 8, TOK // 2)
    exchange(3, lambda peer: gmsg.at[peer], lambda k: grcv.at[k - 1], "tp")
    for copy in pending:
        copy.wait_send()
    for sem, blocks in ((zs_s, 3), (ys_s, 12)):
        ref = wb.at[pl.ds(0, blocks)]
        remote(ref, ref, sem, sem, dp, tp ^ 1).wait_send()
    exchanged(3, grcv)
    total = gmsg[tp]
    for k in range(N - 1):
        total = total + grcv[k]
    by_example(gmat, jnp.concatenate([total[0:4, :], total[4:8, :]], axis=1))
    t1 = dot_nt(gmat[...], iph2(), HIGHEST)
    _, lane = iota2((16, 128))
    both = jnp.where(((lane >> 2) & 1) == 0, t1, t2[...])
    row, col = iota2((128, 128))
    feature = ((row >> 3) << 2) + (row & 3)
    wanted = ((col >> 3) << 1) + (col & 1)
    erow, lane = iota2((16, 128))
    for half in range(2):
        place = jnp.where(feature == wanted + 32 * half, 1.0, 0.0)
        moved = dot(both, place, HIGHEST)
        moved = jnp.where((erow >> 2) == ((lane >> 1) & 3), moved, 0.0)
        pall[dp, 4 * half : 4 * half + 4, :] = (
            moved[0:4, :] + moved[4:8, :] + moved[8:12, :] + moved[12:16, :]
        )
    exchange(4, lambda peer: pall.at[dp], lambda k: pall.at[dp], "dp")
    exchanged(4, pall.at[pl.ds(0, N - 1)])
    sketch = pall[...].reshape(128, 128)
    hi, lo = split(sketch)
    squares = dot_nt(jnp.ones((8, 128), jnp.float32), sketch * sketch, HIGHEST)
    r = []
    for jh in range(2):
        qq = qj[:, :, 128 * jh : 128 * jh + 128].reshape(N * 32, 128)
        r.append(dot_nt(qq, hi) + dot_nt(qq, lo))
    _, lane = iota2((N * 32, 128))
    part = jnp.where(((lane >> 2) & 1) == 0, r[0], r[1])
    down = (part + pltpu.roll(part, 124, 1)).reshape(N, 32, 128)
    up = (part + pltpu.roll(part, 4, 1)).reshape(N, 32, 128)
    _, lane = iota2((16, 128))
    scm[:, 0:16, :] = jnp.where((((lane >> 2) & 1) == 0)[None], down[:, 0:16, :], up[:, 16:32, :])
    scm[:, 16:24, :] = jnp.broadcast_to(squares[None], (N, 8, 128))
    exchange(5, lambda peer: scm.at[peer], lambda k: scr.at[k - 1], "tp")
    exchanged(5, scr)
    total = scm[tp]
    for k in range(N - 1):
        total = total + scr[k]
    row, col = iota2((64, 128))
    pick = jnp.where(((row >> 2) == (col >> 3)) & ((row & 3) == (col & 3)), 1.0, 0.0)
    square = dot_nt(total[16:24, :], pick, HIGHEST)[0:1, :]
    scale = lax.rsqrt(square * (1.0 / 4096.0) + 1e-06) * (1.0 / 64.0)
    for half in range(2):
        here = jnp.where(((col >> 2) & 1) == half, pick, 0.0)
        out_ref[16 * half : 16 * half + 16, :] = dot_nt(total[0:16, :], here, HIGHEST) * scale


def local(
    inputs, gate_pre, up_pre, out_grads, down_weight, example_ids,
    input_factor, gate_factor, up_factor, hidden_factor, output_factor, queries,
):
    hbm = pl.BlockSpec(memory_space=pl.ANY)
    vmem = pl.BlockSpec(memory_space=pltpu.VMEM)
    bf16, f32 = jnp.bfloat16, jnp.float32
    dma = pltpu.SemaphoreType.DMA
    return pl.pallas_call(
        kernel,
        out_shape=jax.ShapeDtypeStruct((32, 64), f32),
        in_specs=[hbm, hbm, hbm, hbm, hbm, vmem, vmem, vmem, vmem, vmem, hbm, hbm],
        out_specs=vmem,
        scratch_shapes=[
            pltpu.VMEM((N, TOK, DS), bf16),
            pltpu.VMEM((N, FS, DS), bf16),
            pltpu.VMEM((TOK, DS), bf16),
            pltpu.VMEM((TOK, FS), bf16),
            pltpu.VMEM((TOK, FS), bf16),
            pltpu.VMEM((64, N * DS), bf16),
            pltpu.VMEM((32, 4096), bf16),
            pltpu.VMEM((N, 256, 128), f32),
            pltpu.VMEM((N, 32, 256), bf16),
            pltpu.VMEM((NCH, TOK, 2 * CH), f32),
            pltpu.VMEM((2, NCH, 128, 2 * CH), bf16),
            pltpu.VMEM((TOK, 128), f32),
            pltpu.VMEM((TOK, 2 * CH), f32),
            pltpu.VMEM((N, 8, TOK), f32),
            pltpu.VMEM((N - 1, 8, TOK), f32),
            pltpu.VMEM((N, 8, TOK), f32),
            pltpu.VMEM((N, 8, TOK), f32),
            pltpu.VMEM((16, TOK), f32),
            pltpu.VMEM((16, TOK), f32),
            pltpu.VMEM((16, 128), f32),
            pltpu.VMEM((TOK // 2, 128), f32),
            pltpu.VMEM((N, 8, TOK // 2), f32),
            pltpu.VMEM((N - 1, 8, TOK // 2), f32),
            pltpu.VMEM((N, 8, 128), f32),
            pltpu.VMEM((N, 32, 256), bf16),
            pltpu.VMEM((N, 24, 128), f32),
            pltpu.VMEM((N - 1, 24, 128), f32),
            dma((7,)),
            dma,
            dma((4 * NCH,)),
            dma,
            dma((16 * NCH,)),
            dma,
            dma,
            dma((8,)),
            dma((8,)),
            dma((8,)),
            dma((8,)),
            dma((6,)),
            dma((6,)),
        ],
        compiler_params=pltpu.CompilerParams(
            collective_id=0, has_side_effects=True, vmem_limit_bytes=60 * 1024 * 1024
        ),
        cost_estimate=pl.CostEstimate(
            flops=2 * TOK * FS * N * DS, bytes_accessed=8 * 1024 * 1024, transcendentals=TOK * FS
        ),
        name="gather_and_score",
    )(
        inputs, gate_pre, up_pre, out_grads, down_weight, example_ids,
        input_factor.T, gate_factor.T, up_factor.T, hidden_factor.T, output_factor.T, queries,
    ).T


def solution(mesh):
    return jax.shard_map(
        local,
        mesh=mesh,
        in_specs=(
            P("dp", "tp"),
            P("dp", "tp"),
            P("dp", "tp"),
            P("dp", "tp"),
            P("tp", "dp"),
            P("dp"),
            P("tp", None),
            P("tp", None),
            P("tp", None),
            P("tp", None),
            P(),
            P(("dp", "tp"), None),
        ),
        out_specs=P(None, ("dp", "tp")),
        check_vma=False,
    )
```
